32 devices in a mesh: row: 4 (over z), col: 4 (over y, x), dep: 2 (over core).
Axes of the slice: x: 2, y: 2, z: 4, core: 2. Of those that a mesh axis runs over, the one named last changes fastest.
Arguments:
- load: float32 [3, 8, 32, 32, 1024], P(None, None, 'row', 'col', 'dep'), may hold values from -6 to 6
- diagonal_block: float32 [3, 3, 32, 32, 1024], P(None, None, 'row', 'col', 'dep'), may hold values from -0.3 to 12, as said below
- coupling: float32 [6, 3, 3, 32, 32, 1024], P(None, None, None, 'row', 'col', 'dep'), may hold values from -0.15 to 0.15
- aggregates: int32 [32, 32, 1024], P('row', 'col', 'dep'), may hold values from 0 to 63, as said below
- coarse_inverse: float32 [4, 2, 768, 768], P('col', 'dep'), may hold values from -0.02 to 0.03
Outputs:
- correction: float32 [3, 8, 32, 32, 1024], P(None, None, 'row', 'col', 'dep')
The draws below stay inside these ranges and needn't reach their ends.
Inputs may be any that keep to these rules, and one draw needn't show every extreme that they name: Each device's nodes form 64 nonempty aggregates of nearby nodes, numbered locally. `diagonal_block`: diagonally dominant blocks with positive diagonal.
All inputs are finite; a program needn't handle non-finite values.
Results may differ from the reference program's by a relative error of at most 0.00005.
Values sent between devices are 32-bit elements; how exact they have to be, the bound alone decides.
A program may use at most 128 MiB of HBM per device.

```python
import jax
import jax.numpy as jnp
from jax import lax

CX = 8
CY = 8
CZ = 512
RHS = 8
AGG = 64
AZ = 32
NCG = 768
NX = 32
NY = 32
NZ = 1024
N_ROW = 4
N_COL = 4
N_DEP = 2


def draw_aggregates(key, part):
    lx = jnp.arange(NX, dtype=jnp.int32) % CX
    ly = jnp.arange(NY, dtype=jnp.int32) % CY
    lz = jnp.arange(NZ, dtype=jnp.int32) % CZ
    base = (lx[:, None, None] // 4 * (CY // 4) + ly[None, :, None] // 4) * 16 + lz[None, None, :] // AZ
    flips = jax.random.randint(jax.random.fold_in(key, 11), (NX, NY, NZ), 0, 2).astype(jnp.int32)
    movable = jnp.logical_and(lz % AZ == 0, lz >= AZ)[None, None, :]
    moved = jnp.where(jnp.logical_and(movable, flips == 1), base - 1, base)
    return moved.astype(jnp.int32)


def draw_diagonal_block(key, part):
    values = 4.0 * jnp.exp(jax.random.uniform(jax.random.fold_in(key, 3), (3, NX, NY, NZ), jnp.float32) * 1.0986)
    off = jax.random.uniform(jax.random.fold_in(key, 5), (3, 3, NX, NY, NZ), jnp.float32, -0.3, 0.3)
    eye = jnp.eye(3, dtype=jnp.float32)[:, :, None, None, None]
    diag = values[:, None] * jnp.eye(3, dtype=jnp.float32)[:, :, None, None, None]
    return diag + (1.0 - eye) * off


def draw_coarse_inverse(key, part):
    noise = jnp.clip(0.002 * jax.random.normal(jax.random.fold_in(key, 7), (N_COL, N_DEP, NCG, NCG), jnp.float32), -0.02, 0.02)
    return noise + 0.01 * jnp.eye(NCG, dtype=jnp.float32)[None, None]


def level_of(stream_key, dims, split, low, largest):
    level = 1.0
    for position, blocks in split:
        heights = jax.random.uniform(jax.random.fold_in(jax.random.fold_in(stream_key, 6), position), (blocks,), jnp.float32, low / len(split), largest / len(split))
        level = level * jnp.repeat(jnp.exp(heights), dims[position] // blocks).reshape((-1,) + (1,) * (len(dims) - 1 - position))
    return level


def centred(stream_key, dims, scale, bound, shards=(), kind=jnp.bfloat16):
    loudness = level_of(stream_key, dims, shards, -0.22, 0.18) if shards else 1.0
    entries = jax.random.normal(stream_key, dims, jnp.float32) * scale * loudness
    return jnp.minimum(jnp.maximum(entries, -bound), bound).astype(kind)


def setup_inputs(seed: int = 0) -> dict:
    seeds = jax.random.split(jax.random.key(seed), 6)
    load = centred(seeds[0], (3, RHS, NX, NY, NZ), 1.0, 6.0, ((2, 4), (3, 4), (4, 2)), jnp.float32)
    diagonal_block = draw_diagonal_block(jax.random.fold_in(seeds[5], 71), 0)
    coupling = jnp.clip(jax.random.uniform(seeds[2], (6, 3, 3, NX, NY, NZ), jnp.float32, -0.15, 0.15) * level_of(seeds[2], (6, 3, 3, NX, NY, NZ), ((3, 4), (4, 4), (5, 2)), -0.4, 0.0), -0.15, 0.15)
    aggregates = draw_aggregates(jax.random.fold_in(seeds[5], 71), 0)
    coarse_inverse = draw_coarse_inverse(jax.random.fold_in(seeds[5], 71), 0)
    return {"load": load, "diagonal_block": diagonal_block, "coupling": coupling, "aggregates": aggregates, "coarse_inverse": coarse_inverse}


def apply_block(matrix, field):
    total = matrix[:, 0][:, None] * field[0][None]
    total = total + matrix[:, 1][:, None] * field[1][None]
    total = total + matrix[:, 2][:, None] * field[2][None]
    return total


def operate(field, padded, diagonal_block, coupling):
    beside_all = [padded[:, :, 2:, 1:-1, 1:-1], padded[:, :, :-2, 1:-1, 1:-1],
              padded[:, :, 1:-1, 2:, 1:-1], padded[:, :, 1:-1, :-2, 1:-1],
              padded[:, :, 1:-1, 1:-1, 2:], padded[:, :, 1:-1, 1:-1, :-2]]
    total = apply_block(diagonal_block, field)
    for direction in range(6):
        total = total - apply_block(coupling[direction], beside_all[direction])
    return total


def apply_full(field, diagonal_block, coupling):
    padded = jnp.pad(field, ((0, 0), (0, 0), (1, 1), (1, 1), (1, 1)))
    return operate(field, padded, diagonal_block, coupling)


def reference(load, diagonal_block, coupling, aggregates, coarse_inverse):
    weight = 0.8 / jnp.stack([diagonal_block[0, 0], diagonal_block[1, 1], diagonal_block[2, 2]])[:, None]
    first = weight * load
    second = first + weight * (load - apply_full(first, diagonal_block, coupling))
    residual = load - apply_full(second, diagonal_block, coupling)
    ix = jnp.arange(NX, dtype=jnp.int32) // CX
    iy = jnp.arange(NY, dtype=jnp.int32) // CY
    iz = jnp.arange(NZ, dtype=jnp.int32) // CZ
    owner = (ix[:, None, None] * N_COL + iy[None, :, None]) * N_DEP + iz[None, None, :]
    segment = (owner * AGG + aggregates).reshape(-1).astype(jnp.int32)
    count = N_ROW * N_COL * N_DEP * AGG
    flat = residual.reshape(3 * RHS, -1).T
    summed = jax.ops.segment_sum(flat, segment, num_segments=count)
    summed = summed.reshape(N_ROW, N_COL, N_DEP, AGG, 3, RHS).transpose(1, 2, 0, 4, 3, 5)
    coarse_rhs = summed.reshape(N_COL, N_DEP, NCG, RHS)
    coarse_sol = jnp.einsum("cdkl,cdln->cdkn", coarse_inverse, coarse_rhs, precision=lax.Precision.HIGHEST)
    back = coarse_sol.reshape(N_COL, N_DEP, N_ROW, 3, AGG, RHS).transpose(2, 0, 1, 4, 3, 5)
    back = back.reshape(count, 3 * RHS)
    spread = jnp.take(back, segment, axis=0).T.reshape(3, RHS, NX, NY, NZ)
    third = second + spread
    return third + weight * (load - apply_full(third, diagonal_block, coupling))
```

```python
import functools

import jax
import jax.numpy as jnp
from jax import lax
from jax.experimental import pallas as pl
from jax.experimental.pallas import tpu as pltpu
from jax.sharding import PartitionSpec as P

LANES = 128
SUB = 8
MESH = pl.DeviceIdType.MESH


def kernel(
    n_row, n_col, agg,
    load_h, diag_h, coup_h, aggr_h, inv_h, out_h,
    load_v, diag_v, coup, ag, inv, wgt, first, second, resid, third, out_v,
    xh, yh, ys, agx, agy, agys, agz, gath, tabs,
    in_sem, send_sem, recv_sem, g_send, g_recv, out_sem,
):
    rhs, xs = load_v.shape[1], load_v.shape[2]
    zts = load_v.shape[4] // LANES
    rows = 3 * rhs * SUB
    rb = 4
    row, col, dep = lax.axis_index("row"), lax.axis_index("col"), lax.axis_index("dep")
    other = 1 - dep
    own_rows = 3 * agg

    copies = [
        pltpu.make_async_copy(diag_h, diag_v, in_sem.at[0]),
        pltpu.make_async_copy(load_h, load_v, in_sem.at[1]),
        pltpu.make_async_copy(aggr_h, ag, in_sem.at[2]),
        pltpu.make_async_copy(coup_h, coup, in_sem.at[3]),
        pltpu.make_async_copy(
            inv_h.at[0, 0, pl.ds(pl.multiple_of(row * own_rows, SUB), own_rows), :], inv, in_sem.at[4]
        ),
    ]
    for copy in copies:
        copy.start()

    sides = [
        (row > 0, {"row": row - 1}),
        (row < n_row - 1, {"row": row + 1}),
        (col > 0, {"col": col - 1}),
        (col < n_col - 1, {"col": col + 1}),
    ]
    barrier = pltpu.get_barrier_semaphore()
    for step in range(1, n_row):
        pl.semaphore_signal(barrier, inc=1, device_id={"row": lax.rem(row + step, n_row)}, device_id_type=MESH)
    for has, device in sides[2:]:
        @pl.when(has)
        def _():
            pl.semaphore_signal(barrier, inc=1, device_id=device, device_id_type=MESH)
    pl.semaphore_signal(barrier, inc=1, device_id={"dep": other}, device_id_type=MESH)

    def zlane(zt):
        return pl.ds(pl.multiple_of(zt * LANES, LANES), LANES)

    def zero_edges(field):
        def body(zt, _):
            field[0, zt + 1] = jnp.zeros((rows, LANES), jnp.float32)
            field[xs + 1, zt + 1] = jnp.zeros((rows, LANES), jnp.float32)
            return 0

        lax.fori_loop(0, zts, body, 0)
        side = dep * (zts + 1)

        def body_z(x, _):
            field[x + 1, side] = jnp.zeros((rows, LANES), jnp.float32)
            return 0

        lax.fori_loop(0, xs, body_z, 0)

    zero_edges(first)
    copies[0].wait()
    copies[1].wait()

    def scale(x, _):
        for c in range(3):
            wgt[c, x] = 0.8 / diag_v[c, c, x]

        def inner(zt, _):
            for c in range(3):
                value = wgt[c, x, :, zlane(zt)][None] * load_v[c, :, x, :, zlane(zt)]
                first[x + 1, zt + 1, c * rhs * SUB:(c + 1) * rhs * SUB, :] = value.reshape(rhs * SUB, LANES)
            return 0

        lax.fori_loop(0, zts, inner, 0)
        return 0

    lax.fori_loop(0, xs, scale, 0)

    def pack_y(field, slot):
        def body(i, _):
            x, zt = i // zts, i % zts
            for s in range(2):
                ys[slot, s, x, zt] = field[x + 1, zt + 1, pl.ds(s * (SUB - 1), 3 * rhs, stride=SUB), :]
            return 0

        lax.fori_loop(0, xs * zts, body, 0)

    def remote(src, dst, sem, device):
        return pltpu.make_async_remote_copy(
            src_ref=src, dst_ref=dst, send_sem=send_sem.at[sem], recv_sem=recv_sem.at[sem],
            device_id=device, device_id_type=MESH,
        )

    def to_sides(base, pieces):
        found = []
        for s, (has, device) in enumerate(sides):
            src, dst = pieces[s]
            found.append((has, remote(src, dst, base + (s ^ 1), device)))
        return found

    def from_sides(base, pieces):
        found = []
        for s, (has, device) in enumerate(sides):
            src, dst = pieces[s ^ 1]
            found.append((has, remote(src, dst, base + s, device)))
        return found

    def start_all(found, only=range(4)):
        for s in only:
            has, copy = found[s]
            pl.when(has)(copy.start)

    def wait_sends(found):
        for has, copy in found:
            pl.when(has)(copy.wait_send)

    def face_pieces(field, slot):
        return [
            (field.at[1, pl.ds(1, zts)], xh.at[slot, 1]),
            (field.at[xs, pl.ds(1, zts)], xh.at[slot, 0]),
            (ys.at[slot, 0], yh.at[slot, 1]),
            (ys.at[slot, 1], yh.at[slot, 0]),
        ]

    own_z = (1 - dep) * (zts - 1) + 1
    halo_z = (1 - dep) * (zts + 1)
    far_z = dep * (zts + 1)

    def z_copy(field, sem):
        return remote(field.at[pl.ds(1, xs), own_z], field.at[pl.ds(1, xs), far_z], sem, {"dep": other})

    pack_y(first, 0)
    pl.semaphore_wait(barrier, n_row - 1 + 1 + (col > 0).astype(jnp.int32) + (col < n_col - 1).astype(jnp.int32))
    p1 = face_pieces(first, 0)
    e1 = to_sides(0, p1)
    start_all(e1, (2, 3, 0, 1))
    z1 = z_copy(first, 4)
    z1.start()

    copies[2].wait()
    for x in range(xs):
        for s in range(2):
            y = s * (SUB - 1)
            agys[s, x:x + 1, :] = ag[x, y:y + 1, :]
    pa = [
        (ag.at[0], agx.at[1]), (ag.at[xs - 1], agx.at[0]),
        (agys.at[0], agy.at[1]), (agys.at[1], agy.at[0]),
    ]
    ea = to_sides(10, pa)
    start_all(ea)
    za = remote(
        ag.at[:, :, zlane((1 - dep) * (zts - 1))], agz, 14, {"dep": other}
    )
    za.start()
    zero_edges(second)
    zero_edges(third)
    tabs[...] = jnp.zeros_like(tabs)
    gath[row] = jnp.zeros((3 * rhs, LANES), jnp.float32)
    copies[3].wait()
    z1.wait_recv()

    lane = lax.broadcasted_iota(jnp.int32, (rb, SUB, LANES), 2)
    sub = lax.broadcasted_iota(jnp.int32, (rb, SUB, LANES), 1)
    at_first, at_last = lane == 0, lane == LANES - 1
    at_top, at_bottom = sub == 0, sub == SUB - 1

    def tile_rows(c, r0):
        return slice((c * rhs + r0) * SUB, (c * rhs + r0 + rb) * SUB)

    def tile(field, x, zt, c, r0):
        return field[x, zt, tile_rows(c, r0), :].reshape(rb, SUB, LANES)

    def operate(field, x, zt, r0):
        own = [tile(field, x + 1, zt + 1, c, r0) for c in range(3)]
        zl = zlane(zt)
        total = []
        for a in range(3):
            t = diag_v[a, 0, x, :, zl][None] * own[0]
            for c in (1, 2):
                t = t + diag_v[a, c, x, :, zl][None] * own[c]
            total.append(t)
        for d in range(6):
            for c in range(3):
                if d == 0:
                    near = tile(field, x + 2, zt + 1, c, r0)
                elif d == 1:
                    near = tile(field, x, zt + 1, c, r0)
                elif d == 2:
                    near = jnp.where(at_bottom, 0.0, pltpu.roll(own[c], SUB - 1, 1))
                elif d == 3:
                    near = jnp.where(at_top, 0.0, pltpu.roll(own[c], 1, 1))
                elif d == 4:
                    near = pltpu.roll(jnp.where(at_first, tile(field, x + 1, zt + 2, c, r0), own[c]), LANES - 1, 2)
                else:
                    near = pltpu.roll(jnp.where(at_last, tile(field, x + 1, zt, c, r0), own[c]), 1, 2)
                for a in range(3):
                    total[a] = total[a] - coup[d, a, c, x, :, zl][None] * near
        return own, total

    def sweep(body):
        def run(i, _):
            x, zt = i // zts, i % zts
            for r0 in range(0, rhs, rb):
                body(x, zt, r0)
            return 0

        lax.fori_loop(0, xs * zts, run, 0)

    def smooth(x, zt, r0):
        own, total = operate(first, x, zt, r0)
        zl = zlane(zt)
        for a in range(3):
            value = own[a] + wgt[a, x, :, zl][None] * (load_v[a, r0:r0 + rb, x, :, zl] - total[a])
            second[x + 1, zt + 1, tile_rows(a, r0), :] = value.reshape(rb * SUB, LANES)

    sweep(smooth)

    def fix_x(field, off, s, slot, weighted):
        x = s * (xs - 1)
        d = 1 - s

        def body(zt, _):
            zl = zlane(zt)
            for r0 in range(0, rhs, rb):
                near = [xh[slot, s, zt, tile_rows(c, r0), :].reshape(rb, SUB, LANES) for c in range(3)]
                for a in range(3):
                    t = coup[d, a, 0, x, :, zl][None] * near[0]
                    for c in (1, 2):
                        t = t + coup[d, a, c, x, :, zl][None] * near[c]
                    t = t.reshape(rb * SUB, LANES)
                    if weighted:
                        t = (wgt[a, x, :, zl][None] * t.reshape(rb, SUB, LANES)).reshape(rb * SUB, LANES)
                        field[x + off, zt + off, tile_rows(a, r0), :] += t
                    else:
                        field[x + off, zt + off, tile_rows(a, r0), :] += t
            return 0

        lax.fori_loop(0, zts, body, 0)

    def fix_y(field, off, s, slot, weighted):
        y = s * (SUB - 1)
        d = 3 - s

        def body(i, _):
            x, zt = i // zts, i % zts
            zl = zlane(zt)
            near = [yh[slot, s, x, zt, c * rhs:(c + 1) * rhs, :] for c in range(3)]
            for a in range(3):
                t = coup[d, a, 0, x, y:y + 1, zl] * near[0]
                for c in (1, 2):
                    t = t + coup[d, a, c, x, y:y + 1, zl] * near[c]
                if weighted:
                    t = wgt[a, x, y:y + 1, zl] * t
                at = pl.ds(a * rhs * SUB + y, rhs, stride=SUB)
                field[x + off, zt + off, at, :] = field[x + off, zt + off, at, :] + t
            return 0

        lax.fori_loop(0, xs * zts, body, 0)

    def fix_arrived(arrivals, field, off, slot, weighted):
        for s, (has, copy) in enumerate(arrivals):
            @pl.when(has)
            def _():
                if copy is not None:
                    copy.wait_recv()
                if s < 2:
                    fix_x(field, off, s, slot, weighted)
                else:
                    fix_y(field, off, s - 2, slot, weighted)

    fix_arrived(from_sides(0, p1), second, 1, 0, True)
    pack_y(second, 1)
    p2 = face_pieces(second, 1)
    e2 = to_sides(5, p2)
    start_all(e2, (2, 3, 0, 1))
    z2 = z_copy(second, 9)
    z2.start()
    z2.wait_recv()

    def defect(x, zt, r0):
        own, total = operate(second, x, zt, r0)
        zl = zlane(zt)
        for a in range(3):
            value = load_v[a, r0:r0 + rb, x, :, zl] - total[a]
            resid[x, zt, tile_rows(a, r0), :] = value.reshape(rb * SUB, LANES)

    sweep(defect)
    copies[4].wait()
    fix_arrived(from_sides(5, p2), resid, 0, 1, False)

    number = lax.broadcasted_iota(jnp.int32, (agg, zts * LANES), 0)

    def restrict(x, total):
        for y in range(SUB):
            value = jnp.concatenate(
                [resid[x, zt, pl.ds(y, 3 * rhs, stride=SUB), :] for zt in range(zts)], axis=1
            )
            high = value.astype(jnp.bfloat16).astype(jnp.float32)
            both = jnp.concatenate([high, value - high], axis=0).astype(jnp.bfloat16)
            member = (ag[x, y:y + 1, :] == number).astype(jnp.float32).astype(jnp.bfloat16)
            total = total + lax.dot_general(
                both, member, (((1,), (1,)), ((), ())), preferred_element_type=jnp.float32
            )
        return total

    sums = lax.fori_loop(0, xs, restrict, jnp.zeros((6 * rhs, agg), jnp.float32))
    gath[row, :, 0:agg] = sums[:3 * rhs] + sums[3 * rhs:]
    gathers = []
    for step in range(1, n_row):
        copy = pltpu.make_async_remote_copy(
            src_ref=gath.at[row], dst_ref=gath.at[row], send_sem=g_send.at[step - 1], recv_sem=g_recv.at[step - 1],
            device_id={"row": lax.rem(row + step, n_row)}, device_id_type=MESH,
        )
        copy.start()
        gathers.append(copy)
    for step in range(1, n_row):
        source = lax.rem(row + n_row - step, n_row)
        pltpu.make_async_remote_copy(
            src_ref=gath.at[source], dst_ref=gath.at[source], send_sem=g_send.at[step - 1],
            recv_sem=g_recv.at[step - 1], device_id={"row": source}, device_id_type=MESH,
        ).wait_recv()
    vector = jnp.concatenate(
        [gath[i, c * rhs:(c + 1) * rhs, 0:agg] for i in range(n_row) for c in range(3)], axis=1
    )
    solved = lax.dot_general(
        vector, inv[...], (((1,), (1,)), ((), ())), precision=lax.Precision.HIGHEST,
        preferred_element_type=jnp.float32,
    )
    for c in range(3):
        tabs[0, c * rhs:(c + 1) * rhs, 0:agg] = solved[:, c * agg:(c + 1) * agg]
    pt = [(tabs.at[0], tabs.at[1 + (s ^ 1)]) for s in range(4)]
    et = to_sides(15, pt)
    start_all(et)
    zt_copy = remote(tabs.at[0], tabs.at[5], 19, {"dep": other})
    zt_copy.start()

    def look(table, index):
        return jnp.take_along_axis(table, index, axis=1, mode="promise_in_bounds")

    def spread(i, _):
        x, zt = i // zts, i % zts
        index = ag[x, :, zlane(zt)]
        for k in range(3 * rhs):
            table = jnp.broadcast_to(tabs[0, k:k + 1, :], (SUB, LANES))
            third[x + 1, zt + 1, k * SUB:(k + 1) * SUB, :] = look(table, index)
        return 0

    lax.fori_loop(0, xs * zts, spread, 0)
    zt_copy.wait_recv()
    za.wait_recv()

    def spread_z(x, _):
        index = agz[x]
        for k in range(3 * rhs):
            table = jnp.broadcast_to(tabs[5, k:k + 1, :], (SUB, LANES))
            third[x + 1, halo_z, k * SUB:(k + 1) * SUB, :] = look(table, index)
        return 0

    lax.fori_loop(0, xs, spread_z, 0)

    def final(x, zt, r0):
        own, total = operate(third, x, zt, r0)
        zl = zlane(zt)
        for a in range(3):
            left = resid[x, zt, tile_rows(a, r0), :].reshape(rb, SUB, LANES) - total[a]
            value = tile(second, x + 1, zt + 1, a, r0) + own[a] + wgt[a, x, :, zl][None] * left
            out_v[x, zt, tile_rows(a, r0), :] = value.reshape(rb * SUB, LANES)

    sweep(final)

    arrived_t, arrived_a = from_sides(15, pt), from_sides(10, pa)
    for s in range(4):
        has = sides[s][0]

        @pl.when(has)
        def _():
            arrived_t[s][1].wait_recv()
            arrived_a[s][1].wait_recv()
            if s < 2:
                def body(zt, _):
                    index = agx[s, :, zlane(zt)]
                    for k in range(3 * rhs):
                        table = jnp.broadcast_to(tabs[1 + s, k:k + 1, :], (SUB, LANES))
                        xh[2, s, zt, k * SUB:(k + 1) * SUB, :] = look(table, index)
                    return 0

                lax.fori_loop(0, zts, body, 0)
                fix_x(out_v, 0, s, 2, True)
            else:
                def body(zt, _):
                    for x in range(xs):
                        index = jnp.broadcast_to(agy[s - 2, x:x + 1, zlane(zt)], (SUB, LANES))
                        for c in range(3):
                            yh[2, s - 2, x, zt, c * rhs:(c + 1) * rhs, :] = look(
                                tabs[1 + s, c * rhs:(c + 1) * rhs, :], index
                            )
                    return 0

                lax.fori_loop(0, zts, body, 0)
                fix_y(out_v, 0, s - 2, 2, True)

    outs = []
    for x in range(xs):
        for zt in range(zts):
            outs.append(pltpu.make_async_copy(
                out_v.at[x, zt].reshape(3, rhs, SUB, LANES),
                out_h.at[:, :, x, :, pl.ds(zt * LANES, LANES)],
                out_sem.at[x * zts + zt],
            ))
    for copy in outs:
        copy.start()
    for found in (e1, e2, ea, et):
        wait_sends(found)
    for copy in (z1, z2, za, zt_copy, *gathers):
        copy.wait_send()
    for copy in outs:
        copy.wait()


def on_device(n_row, n_col, load, diagonal_block, coupling, aggregates, coarse_inverse):
    _, rhs, xs, sub, depth = load.shape
    zts = depth // LANES
    ncg = coarse_inverse.shape[-1]
    agg = ncg // n_row // 3
    rows = 3 * rhs * sub
    f32 = jnp.float32
    dma = pltpu.SemaphoreType.DMA
    field = pltpu.VMEM((xs + 2, zts + 2, rows, LANES), f32)
    block = pltpu.VMEM((xs, zts, rows, LANES), f32)
    return pl.pallas_call(
        functools.partial(kernel, n_row, n_col, agg),
        out_shape=jax.ShapeDtypeStruct(load.shape, f32),
        in_specs=[pl.BlockSpec(memory_space=pl.ANY)] * 5,
        out_specs=pl.BlockSpec(memory_space=pl.ANY),
        scratch_shapes=[
            pltpu.VMEM(load.shape, f32),
            pltpu.VMEM(diagonal_block.shape, f32),
            pltpu.VMEM(coupling.shape, f32),
            pltpu.VMEM(aggregates.shape, jnp.int32),
            pltpu.VMEM((3 * agg, ncg), f32),
            pltpu.VMEM((3, xs, sub, depth), f32),
            field, field, block, field, block,
            pltpu.VMEM((3, 2, zts, rows, LANES), f32),
            pltpu.VMEM((3, 2, xs, zts, 3 * rhs, LANES), f32),
            pltpu.VMEM((2, 2, xs, zts, 3 * rhs, LANES), f32),
            pltpu.VMEM((2, sub, depth), jnp.int32),
            pltpu.VMEM((2, xs, depth), jnp.int32),
            pltpu.VMEM((2, xs, depth), jnp.int32),
            pltpu.VMEM((xs, sub, LANES), jnp.int32),
            pltpu.VMEM((n_row, 3 * rhs, LANES), f32),
            pltpu.VMEM((6, 3 * rhs, LANES), f32),
            dma((5,)),
            dma((20,)),
            dma((20,)),
            dma((n_row - 1,)),
            dma((n_row - 1,)),
            dma((xs * zts,)),
        ],
        compiler_params=pltpu.CompilerParams(
            collective_id=0, has_side_effects=True, vmem_limit_bytes=60 * 2**20
        ),
    )(load, diagonal_block, coupling, aggregates, coarse_inverse)


def solution(mesh):
    in_specs = (
        P(None, None, "row", "col", "dep"),
        P(None, None, "row", "col", "dep"),
        P(None, None, None, "row", "col", "dep"),
        P("row", "col", "dep"),
        P("col", "dep", None, None),
    )
    out_specs = P(None, None, "row", "col", "dep")
    return jax.shard_map(
        functools.partial(on_device, mesh.shape["row"], mesh.shape["col"]),
        mesh=mesh, in_specs=in_specs, out_specs=out_specs, check_vma=False,
    )
```

```python
import functools

import jax
import jax.numpy as jnp
from jax import lax
from jax.experimental import pallas as pl
from jax.experimental.pallas import tpu as pltpu
from jax.sharding import PartitionSpec as P

LANES = 128
SUB = 8
MESH = pl.DeviceIdType.MESH


def kernel(
    n_row, n_col, agg,
    load_h, diag_h, coup_h, aggr_h, inv_h, out_h,
    load_v, diag_v, coup, ag, inv, wgt, first, second, resid, third, out_v,
    xh, yh, ys, relay, agx, agy, agys, agz, gath, tabs,
    in_sem, load_sem, send_sem, recv_sem, y_send, y_recv, r_send, r_recv, g_send, g_recv, out_sem,
):
    rhs, xs = load_v.shape[1], load_v.shape[2]
    zts = load_v.shape[4] // LANES
    rows = 3 * rhs * SUB
    rb = 4
    row, col, dep = lax.axis_index("row"), lax.axis_index("col"), lax.axis_index("dep")
    other = 1 - dep
    own_rows = 3 * agg

    def order(k):
        return jnp.where(k < xs - 2, k + 1, jnp.where(k == xs - 2, 0, xs - 1))

    def load_copy(x):
        return pltpu.make_async_copy(load_h.at[:, :, x], load_v.at[:, :, x], load_sem.at[x])

    diagonal = [
        pltpu.make_async_copy(diag_h.at[c, c], diag_v.at[c, c], in_sem.at[3 * c + c]) for c in range(3)
    ]
    off_diagonal = [
        pltpu.make_async_copy(diag_h.at[a, c], diag_v.at[a, c], in_sem.at[3 * a + c])
        for a in range(3) for c in range(3) if a != c
    ]
    aggr_copy = pltpu.make_async_copy(aggr_h, ag, in_sem.at[9])
    coup_copy = pltpu.make_async_copy(coup_h, coup, in_sem.at[10])
    inv_copy = pltpu.make_async_copy(
        inv_h.at[0, 0, pl.ds(pl.multiple_of(row * own_rows, SUB), own_rows), :], inv, in_sem.at[11]
    )
    for copy in diagonal:
        copy.start()
    for x in [*range(1, xs - 1), 0, xs - 1]:
        load_copy(x).start()
    for copy in (aggr_copy, *off_diagonal, coup_copy, inv_copy):
        copy.start()

    sides = [
        (row > 0, {"row": row - 1}),
        (row < n_row - 1, {"row": row + 1}),
        (col > 0, {"col": col - 1}),
        (col < n_col - 1, {"col": col + 1}),
    ]
    barrier = pltpu.get_barrier_semaphore()
    for step in range(1, n_row):
        pl.semaphore_signal(barrier, inc=1, device_id={"row": lax.rem(row + step, n_row)}, device_id_type=MESH)
    for has, device in sides[2:]:
        @pl.when(has)
        def _():
            pl.semaphore_signal(barrier, inc=1, device_id=device, device_id_type=MESH)
    relays = [(col > 1, {"col": col - 2}), (col < n_col - 2, {"col": col + 2})]
    for has, device in relays:
        @pl.when(has)
        def _():
            pl.semaphore_signal(barrier, inc=1, device_id=device, device_id_type=MESH)
    pl.semaphore_signal(barrier, inc=1, device_id={"dep": other}, device_id_type=MESH)

    def zlane(zt):
        return pl.ds(pl.multiple_of(zt * LANES, LANES), LANES)

    def zero_edges(field):
        def body(zt, _):
            field[0, zt + 1] = jnp.zeros((rows, LANES), jnp.float32)
            field[xs + 1, zt + 1] = jnp.zeros((rows, LANES), jnp.float32)
            return 0

        lax.fori_loop(0, zts, body, 0)
        side = dep * (zts + 1)

        def body_z(x, _):
            field[x + 1, side] = jnp.zeros((rows, LANES), jnp.float32)
            return 0

        lax.fori_loop(0, xs, body_z, 0)

    def remote(src, dst, sem, device):
        return pltpu.make_async_remote_copy(
            src_ref=src, dst_ref=dst, send_sem=send_sem.at[sem], recv_sem=recv_sem.at[sem],
            device_id=device, device_id_type=MESH,
        )

    def to_sides(base, pieces):
        found = []
        for s, (has, device) in enumerate(sides[:len(pieces)]):
            src, dst = pieces[s]
            found.append((has, remote(src, dst, base + (s ^ 1), device)))
        return found

    def from_sides(base, pieces):
        found = []
        for s, (has, device) in enumerate(sides[:len(pieces)]):
            src, dst = pieces[s ^ 1]
            found.append((has, remote(src, dst, base + s, device)))
        return found

    def start_all(found):
        for has, copy in found:
            pl.when(has)(copy.start)

    def wait_sends(found):
        for has, copy in found:
            pl.when(has)(copy.wait_send)

    def face_pieces(field, slot):
        return [
            (field.at[1, pl.ds(1, zts)], xh.at[slot, 1]),
            (field.at[xs, pl.ds(1, zts)], xh.at[slot, 0]),
        ]

    odd = lax.rem(col, 2)
    straight = col + 1 - 2 * odd
    has_across = jnp.where(odd == 1, col < n_col - 1, col > 0)
    across = col - 1 + 2 * odd
    corner = col - 2 + 4 * odd
    passes_on = jnp.where(odd == 1, col > 1, col < n_col - 2)
    pass_to = col + 1 - 2 * odd
    half = xs // 2

    def y_copy(src, dst, send, recv, device):
        return pltpu.make_async_remote_copy(
            src_ref=src, dst_ref=dst, send_sem=send, recv_sem=recv,
            device_id={"col": device}, device_id_type=MESH,
        )

    def straight_copy(slot, k):
        x = order(k)
        return y_copy(ys.at[slot, 1 - odd, x], yh.at[slot, odd, x], y_send.at[slot, 0, k],
                      y_recv.at[slot, odd, x], straight)

    def across_copy(slot, k, part):
        x = order(k)
        if part == 0:
            return y_copy(ys.at[slot, odd, x], relay.at[slot, k // 2], y_send.at[slot, 1, k],
                          r_recv.at[slot, k // 2], corner)
        return y_copy(ys.at[slot, odd, x], yh.at[slot, 1 - odd, x], y_send.at[slot, 1, k],
                      y_recv.at[slot, 1 - odd, x], across)

    def pass_copy(slot, j):
        x = order(2 * j)
        return y_copy(relay.at[slot, j], yh.at[slot, 1 - odd, x], r_send.at[slot, j],
                      y_recv.at[slot, 1 - odd, x], pass_to)

    def pass_on(slot, j):
        @pl.when(passes_on)
        def _():
            across_copy(slot, 2 * j, 0).wait_recv()
            pass_copy(slot, j).start()

    def send_y(slot, k, part):
        @pl.when(has_across)
        def _():
            across_copy(slot, k, part).start()

        straight_copy(slot, k).start()

    def wait_y(slot, s, x):
        y_copy(ys.at[slot, s, x], yh.at[slot, s, x], y_send.at[slot, 0, 0], y_recv.at[slot, s, x],
               straight).wait_recv()

    def pack_y(field, slot, x):
        for zt in range(zts):
            for s in range(2):
                ys[slot, s, x, zt] = field[x + 1, zt + 1, pl.ds(s * (SUB - 1), 3 * rhs, stride=SUB), :]

    own_z = (1 - dep) * (zts - 1) + 1
    halo_z = (1 - dep) * (zts + 1)
    far_z = dep * (zts + 1)

    def z_copy(field, sem):
        return remote(field.at[pl.ds(1, xs), own_z], field.at[pl.ds(1, xs), far_z], sem, {"dep": other})

    waits = [sides[2][0], sides[3][0], relays[0][0], relays[1][0]]
    pl.semaphore_wait(barrier, n_row + sum(has.astype(jnp.int32) for has in waits))
    for copy in diagonal:
        copy.wait()

    def scale(j, _):
        for part in range(2):
            k = 2 * j + part
            x = order(k)
            load_copy(x).wait()
            for c in range(3):
                weight = 0.8 / diag_v[c, c, x]
                wgt[c, x] = weight
                for zt in range(zts):
                    zl = slice(zt * LANES, (zt + 1) * LANES)
                    value = weight[:, zl][None] * load_v[c, :, x, :, zl]
                    first[x + 1, zt + 1, c * rhs * SUB:(c + 1) * rhs * SUB, :] = value.reshape(rhs * SUB, LANES)
            pack_y(first, 0, x)
            send_y(0, k, part)
        return 0

    lax.fori_loop(0, half, scale, 0)
    p1 = face_pieces(first, 0)
    e1 = to_sides(0, p1)
    start_all(e1)
    z1 = z_copy(first, 4)
    z1.start()

    aggr_copy.wait()
    for x in range(xs):
        for s in range(2):
            y = s * (SUB - 1)
            agys[s, x:x + 1, :] = ag[x, y:y + 1, :]
    pa = [
        (ag.at[0], agx.at[1]), (ag.at[xs - 1], agx.at[0]),
        (agys.at[0], agy.at[1]), (agys.at[1], agy.at[0]),
    ]
    ea = to_sides(10, pa)
    start_all(ea)
    za = remote(
        ag.at[:, :, zlane((1 - dep) * (zts - 1))], agz, 14, {"dep": other}
    )
    za.start()
    zero_edges(first)
    zero_edges(second)
    zero_edges(third)
    tabs[...] = jnp.zeros_like(tabs)
    gath[row] = jnp.zeros((3 * rhs, LANES), jnp.float32)
    for copy in (*off_diagonal, coup_copy):
        copy.wait()
    z1.wait_recv()

    lane = lax.broadcasted_iota(jnp.int32, (rb, SUB, LANES), 2)
    sub = lax.broadcasted_iota(jnp.int32, (rb, SUB, LANES), 1)
    at_first, at_last = lane == 0, lane == LANES - 1
    at_top, at_bottom = sub == 0, sub == SUB - 1

    def tile_rows(c, r0):
        return slice((c * rhs + r0) * SUB, (c * rhs + r0 + rb) * SUB)

    def tile(field, x, zt, c, r0):
        return field[x, zt, tile_rows(c, r0), :].reshape(rb, SUB, LANES)

    def operate(field, x, zt, r0):
        own = [tile(field, x + 1, zt + 1, c, r0) for c in range(3)]
        zl = zlane(zt)
        total = []
        for a in range(3):
            t = diag_v[a, 0, x, :, zl][None] * own[0]
            for c in (1, 2):
                t = t + diag_v[a, c, x, :, zl][None] * own[c]
            total.append(t)
        for d in range(6):
            for c in range(3):
                if d == 0:
                    near = tile(field, x + 2, zt + 1, c, r0)
                elif d == 1:
                    near = tile(field, x, zt + 1, c, r0)
                elif d == 2:
                    near = jnp.where(at_bottom, 0.0, pltpu.roll(own[c], SUB - 1, 1))
                elif d == 3:
                    near = jnp.where(at_top, 0.0, pltpu.roll(own[c], 1, 1))
                elif d == 4:
                    near = pltpu.roll(jnp.where(at_first, tile(field, x + 1, zt + 2, c, r0), own[c]), LANES - 1, 2)
                else:
                    near = pltpu.roll(jnp.where(at_last, tile(field, x + 1, zt, c, r0), own[c]), 1, 2)
                for a in range(3):
                    total[a] = total[a] - coup[d, a, c, x, :, zl][None] * near
        return own, total

    def sweep(body, slot=None):
        def run(i, _):
            x, zt = i // zts, i % zts
            for r0 in range(0, rhs, rb):
                body(x, zt, r0)
            return 0

        if slot is None:
            lax.fori_loop(0, xs * zts, run, 0)
            return

        def quarter(j, _):
            lax.fori_loop(2 * zts * j, 2 * zts * (j + 1), run, 0)
            pass_on(slot, j)
            return 0

        lax.fori_loop(0, half, quarter, 0)

    def smooth(x, zt, r0):
        own, total = operate(first, x, zt, r0)
        zl = zlane(zt)
        for a in range(3):
            value = own[a] + wgt[a, x, :, zl][None] * (load_v[a, r0:r0 + rb, x, :, zl] - total[a])
            second[x + 1, zt + 1, tile_rows(a, r0), :] = value.reshape(rb * SUB, LANES)

    sweep(smooth, 0)

    def fix_x(field, off, s, slot, weighted):
        x = s * (xs - 1)
        d = 1 - s

        def body(zt, _):
            zl = zlane(zt)
            for r0 in range(0, rhs, rb):
                near = [xh[slot, s, zt, tile_rows(c, r0), :].reshape(rb, SUB, LANES) for c in range(3)]
                for a in range(3):
                    t = coup[d, a, 0, x, :, zl][None] * near[0]
                    for c in (1, 2):
                        t = t + coup[d, a, c, x, :, zl][None] * near[c]
                    t = t.reshape(rb * SUB, LANES)
                    if weighted:
                        t = (wgt[a, x, :, zl][None] * t.reshape(rb, SUB, LANES)).reshape(rb * SUB, LANES)
                        field[x + off, zt + off, tile_rows(a, r0), :] += t
                    else:
                        field[x + off, zt + off, tile_rows(a, r0), :] += t
            return 0

        lax.fori_loop(0, zts, body, 0)

    def fix_y(field, off, s, slot, weighted, x):
        y = s * (SUB - 1)
        d = 3 - s
        for zt in range(zts):
            zl = slice(zt * LANES, (zt + 1) * LANES)
            near = [yh[slot, s, x, zt, c * rhs:(c + 1) * rhs, :] for c in range(3)]
            for a in range(3):
                t = coup[d, a, 0, x, y:y + 1, zl] * near[0]
                for c in (1, 2):
                    t = t + coup[d, a, c, x, y:y + 1, zl] * near[c]
                if weighted:
                    t = wgt[a, x, y:y + 1, zl] * t
                at = pl.ds(a * rhs * SUB + y, rhs, stride=SUB)
                field[x + off, zt + off, at, :] = field[x + off, zt + off, at, :] + t

    def fix_x_arrived(arrivals, field, off, slot, weighted):
        for s, (has, copy) in enumerate(arrivals):
            @pl.when(has)
            def _():
                copy.wait_recv()
                fix_x(field, off, s, slot, weighted)

    def fix_y_arrived(field, off, slot, weighted, x):
        for s in range(2):
            @pl.when(sides[2 + s][0])
            def _():
                wait_y(slot, s, x)
                fix_y(field, off, s, slot, weighted, x)

    def renew(j, _):
        @pl.when(j == half - 1)
        def _():
            fix_x_arrived(from_sides(0, p1), second, 1, 0, True)

        for part in range(2):
            k = 2 * j + part
            x = order(k)
            fix_y_arrived(second, 1, 0, True, x)
            pack_y(second, 1, x)
            send_y(1, k, part)
        return 0

    lax.fori_loop(0, half, renew, 0)
    p2 = face_pieces(second, 1)
    e2 = to_sides(5, p2)
    start_all(e2)
    z2 = z_copy(second, 9)
    z2.start()
    z2.wait_recv()

    def defect(x, zt, r0):
        own, total = operate(second, x, zt, r0)
        zl = zlane(zt)
        for a in range(3):
            value = load_v[a, r0:r0 + rb, x, :, zl] - total[a]
            resid[x, zt, tile_rows(a, r0), :] = value.reshape(rb * SUB, LANES)

    sweep(defect, 1)

    number = lax.broadcasted_iota(jnp.int32, (agg, zts * LANES), 0)

    def restrict(x, total, lines):
        for y in lines:
            value = jnp.concatenate(
                [resid[x, zt, pl.ds(y, 3 * rhs, stride=SUB), :] for zt in range(zts)], axis=1
            )
            high = value.astype(jnp.bfloat16).astype(jnp.float32)
            both = jnp.concatenate([high, value - high], axis=0).astype(jnp.bfloat16)
            member = (ag[x, y:y + 1, :] == number).astype(jnp.float32).astype(jnp.bfloat16)
            total = total + lax.dot_general(
                both, member, (((1,), (1,)), ((), ())), preferred_element_type=jnp.float32
            )
        return total

    inner = range(1, SUB - 1)
    sums = lax.fori_loop(
        1, xs - 1, lambda x, total: restrict(x, total, inner), jnp.zeros((6 * rhs, agg), jnp.float32)
    )

    def finish(k, total):
        x = order(k)
        fix_y_arrived(resid, 0, 1, False, x)
        return restrict(x, total, (0, SUB - 1))

    sums = lax.fori_loop(0, xs - 2, finish, sums)
    fix_x_arrived(from_sides(5, p2), resid, 0, 1, False)

    def finish_edge(k, total):
        x = order(k)
        total = restrict(x, total, inner)
        fix_y_arrived(resid, 0, 1, False, x)
        return restrict(x, total, (0, SUB - 1))

    sums = lax.fori_loop(xs - 2, xs, finish_edge, sums)
    inv_copy.wait()
    gath[row, :, 0:agg] = sums[:3 * rhs] + sums[3 * rhs:]
    gathers = []
    for step in range(1, n_row):
        copy = pltpu.make_async_remote_copy(
            src_ref=gath.at[row], dst_ref=gath.at[row], send_sem=g_send.at[step - 1], recv_sem=g_recv.at[step - 1],
            device_id={"row": lax.rem(row + step, n_row)}, device_id_type=MESH,
        )
        copy.start()
        gathers.append(copy)
    for step in range(1, n_row):
        source = lax.rem(row + n_row - step, n_row)
        pltpu.make_async_remote_copy(
            src_ref=gath.at[source], dst_ref=gath.at[source], send_sem=g_send.at[step - 1],
            recv_sem=g_recv.at[step - 1], device_id={"row": source}, device_id_type=MESH,
        ).wait_recv()
    vector = jnp.concatenate(
        [gath[i, c * rhs:(c + 1) * rhs, 0:agg] for i in range(n_row) for c in range(3)], axis=1
    )
    solved = lax.dot_general(
        vector, inv[...], (((1,), (1,)), ((), ())), precision=lax.Precision.HIGHEST,
        preferred_element_type=jnp.float32,
    )
    for c in range(3):
        tabs[0, c * rhs:(c + 1) * rhs, 0:agg] = solved[:, c * agg:(c + 1) * agg]
    pt = [(tabs.at[0], tabs.at[1 + (s ^ 1)]) for s in range(4)]
    et = to_sides(15, pt)
    start_all(et)
    zt_copy = remote(tabs.at[0], tabs.at[5], 19, {"dep": other})
    zt_copy.start()

    def look(table, index):
        return jnp.take_along_axis(table, index, axis=1, mode="promise_in_bounds")

    def spread(i, _):
        x, zt = i // zts, i % zts
        index = ag[x, :, zlane(zt)]
        for k in range(3 * rhs):
            table = jnp.broadcast_to(tabs[0, k:k + 1, :], (SUB, LANES))
            third[x + 1, zt + 1, k * SUB:(k + 1) * SUB, :] = look(table, index)
        return 0

    lax.fori_loop(0, xs * zts, spread, 0)
    zt_copy.wait_recv()
    za.wait_recv()

    def spread_z(x, _):
        index = agz[x]
        for k in range(3 * rhs):
            table = jnp.broadcast_to(tabs[5, k:k + 1, :], (SUB, LANES))
            third[x + 1, halo_z, k * SUB:(k + 1) * SUB, :] = look(table, index)
        return 0

    lax.fori_loop(0, xs, spread_z, 0)

    def final(x, zt, r0):
        own, total = operate(third, x, zt, r0)
        zl = zlane(zt)
        for a in range(3):
            left = resid[x, zt, tile_rows(a, r0), :].reshape(rb, SUB, LANES) - total[a]
            value = tile(second, x + 1, zt + 1, a, r0) + own[a] + wgt[a, x, :, zl][None] * left
            out_v[x, zt, tile_rows(a, r0), :] = value.reshape(rb * SUB, LANES)

    sweep(final)

    arrived_t, arrived_a = from_sides(15, pt), from_sides(10, pa)
    for s in range(4):
        has = sides[s][0]

        @pl.when(has)
        def _():
            arrived_t[s][1].wait_recv()
            arrived_a[s][1].wait_recv()
            if s < 2:
                def body(zt, _):
                    index = agx[s, :, zlane(zt)]
                    for k in range(3 * rhs):
                        table = jnp.broadcast_to(tabs[1 + s, k:k + 1, :], (SUB, LANES))
                        xh[2, s, zt, k * SUB:(k + 1) * SUB, :] = look(table, index)
                    return 0

                lax.fori_loop(0, zts, body, 0)
                fix_x(out_v, 0, s, 2, True)
            else:
                for x in range(xs):
                    for zt in range(zts):
                        zl = slice(zt * LANES, (zt + 1) * LANES)
                        index = jnp.broadcast_to(agy[s - 2, x:x + 1, zl], (SUB, LANES))
                        for c in range(3):
                            yh[2, s - 2, x, zt, c * rhs:(c + 1) * rhs, :] = look(
                                tabs[1 + s, c * rhs:(c + 1) * rhs, :], index
                            )

                def body_y(x, _):
                    fix_y(out_v, 0, s - 2, 2, True, x)
                    return 0

                lax.fori_loop(0, xs, body_y, 0)

    outs = []
    for x in range(xs):
        for zt in range(zts):
            outs.append(pltpu.make_async_copy(
                out_v.at[x, zt].reshape(3, rhs, SUB, LANES),
                out_h.at[:, :, x, :, pl.ds(zt * LANES, LANES)],
                out_sem.at[x * zts + zt],
            ))
    for copy in outs:
        copy.start()
    for found in (e1, e2, ea, et):
        wait_sends(found)
    for copy in (z1, z2, za, zt_copy, *gathers):
        copy.wait_send()

    def wait_y_sends(j, _):
        for slot in range(2):
            for part in range(2):
                straight_copy(slot, 2 * j + part).wait_send()

                @pl.when(has_across)
                def _():
                    across_copy(slot, 2 * j + part, part).wait_send()

            @pl.when(passes_on)
            def _():
                pass_copy(slot, j).wait_send()
        return 0

    lax.fori_loop(0, half, wait_y_sends, 0)
    for copy in outs:
        copy.wait()


def on_device(n_row, n_col, load, diagonal_block, coupling, aggregates, coarse_inverse):
    _, rhs, xs, sub, depth = load.shape
    zts = depth // LANES
    ncg = coarse_inverse.shape[-1]
    agg = ncg // n_row // 3
    rows = 3 * rhs * sub
    f32 = jnp.float32
    dma = pltpu.SemaphoreType.DMA
    field = pltpu.VMEM((xs + 2, zts + 2, rows, LANES), f32)
    block = pltpu.VMEM((xs, zts, rows, LANES), f32)
    return pl.pallas_call(
        functools.partial(kernel, n_row, n_col, agg),
        out_shape=jax.ShapeDtypeStruct(load.shape, f32),
        in_specs=[pl.BlockSpec(memory_space=pl.ANY)] * 5,
        out_specs=pl.BlockSpec(memory_space=pl.ANY),
        scratch_shapes=[
            pltpu.VMEM(load.shape, f32),
            pltpu.VMEM(diagonal_block.shape, f32),
            pltpu.VMEM(coupling.shape, f32),
            pltpu.VMEM(aggregates.shape, jnp.int32),
            pltpu.VMEM((3 * agg, ncg), f32),
            pltpu.VMEM((3, xs, sub, depth), f32),
            field, field, block, field, block,
            pltpu.VMEM((3, 2, zts, rows, LANES), f32),
            pltpu.VMEM((3, 2, xs, zts, 3 * rhs, LANES), f32),
            pltpu.VMEM((2, 2, xs, zts, 3 * rhs, LANES), f32),
            pltpu.VMEM((2, xs // 2, zts, 3 * rhs, LANES), f32),
            pltpu.VMEM((2, sub, depth), jnp.int32),
            pltpu.VMEM((2, xs, depth), jnp.int32),
            pltpu.VMEM((2, xs, depth), jnp.int32),
            pltpu.VMEM((xs, sub, LANES), jnp.int32),
            pltpu.VMEM((n_row, 3 * rhs, LANES), f32),
            pltpu.VMEM((6, 3 * rhs, LANES), f32),
            dma((12,)),
            dma((xs,)),
            dma((20,)),
            dma((20,)),
            dma((2, 2, xs)),
            dma((2, 2, xs)),
            dma((2, xs // 2)),
            dma((2, xs // 2)),
            dma((n_row - 1,)),
            dma((n_row - 1,)),
            dma((xs * zts,)),
        ],
        compiler_params=pltpu.CompilerParams(
            collective_id=0, has_side_effects=True, vmem_limit_bytes=60 * 2**20
        ),
    )(load, diagonal_block, coupling, aggregates, coarse_inverse)


def solution(mesh):
    in_specs = (
        P(None, None, "row", "col", "dep"),
        P(None, None, "row", "col", "dep"),
        P(None, None, None, "row", "col", "dep"),
        P("row", "col", "dep"),
        P("col", "dep", None, None),
    )
    out_specs = P(None, None, "row", "col", "dep")
    return jax.shard_map(
        functools.partial(on_device, mesh.shape["row"], mesh.shape["col"]),
        mesh=mesh, in_specs=in_specs, out_specs=out_specs, check_vma=False,
    )
```

```python
import functools

import jax
import jax.numpy as jnp
from jax import lax
from jax.experimental import pallas as pl
from jax.experimental.pallas import tpu as pltpu
from jax.sharding import PartitionSpec as P

LANES = 128
SUB = 8
MESH = pl.DeviceIdType.MESH


def kernel(
    n_row, n_col, agg,
    load_h, diag_h, coup_h, aggr_h, inv_h, out_v,
    load_v, diag_v, coup, ag, inv, wgt, first, second, resid, third,
    xh, yh, ys, relay, agx, agy, agys, agz, gath, tabs,
    in_sem, load_sem, send_sem, recv_sem, y_send, y_recv, r_send, r_recv, g_send, g_recv,
):
    rhs, xs = load_v.shape[1], load_v.shape[2]
    zts = load_v.shape[4] // LANES
    rows = 3 * rhs * SUB
    rb = 4
    row, col, dep = lax.axis_index("row"), lax.axis_index("col"), lax.axis_index("dep")
    other = 1 - dep
    own_rows = 3 * agg

    def order(k):
        return jnp.where(k < xs - 2, k + 1, jnp.where(k == xs - 2, 0, xs - 1))

    def load_copy(x):
        return pltpu.make_async_copy(load_h.at[:, :, x], load_v.at[:, :, x], load_sem.at[x])

    diagonal = [
        pltpu.make_async_copy(diag_h.at[c, c], diag_v.at[c, c], in_sem.at[3 * c + c]) for c in range(3)
    ]
    off_diagonal = [
        pltpu.make_async_copy(diag_h.at[a, c], diag_v.at[a, c], in_sem.at[3 * a + c])
        for a in range(3) for c in range(3) if a != c
    ]
    aggr_copy = pltpu.make_async_copy(aggr_h, ag, in_sem.at[9])
    coup_copy = pltpu.make_async_copy(coup_h, coup, in_sem.at[10])
    inv_copy = pltpu.make_async_copy(
        inv_h.at[0, 0, pl.ds(pl.multiple_of(row * own_rows, SUB), own_rows), :], inv, in_sem.at[11]
    )
    for copy in diagonal:
        copy.start()
    for x in [*range(1, xs - 1), 0, xs - 1]:
        load_copy(x).start()
    for copy in (aggr_copy, *off_diagonal, coup_copy, inv_copy):
        copy.start()

    sides = [
        (row > 0, {"row": row - 1}),
        (row < n_row - 1, {"row": row + 1}),
        (col > 0, {"col": col - 1}),
        (col < n_col - 1, {"col": col + 1}),
    ]
    barrier = pltpu.get_barrier_semaphore()
    for step in range(1, n_row):
        pl.semaphore_signal(barrier, inc=1, device_id={"row": lax.rem(row + step, n_row)}, device_id_type=MESH)
    for has, device in sides[2:]:
        @pl.when(has)
        def _():
            pl.semaphore_signal(barrier, inc=1, device_id=device, device_id_type=MESH)
    relays = [(col > 1, {"col": col - 2}), (col < n_col - 2, {"col": col + 2})]
    for has, device in relays:
        @pl.when(has)
        def _():
            pl.semaphore_signal(barrier, inc=1, device_id=device, device_id_type=MESH)
    pl.semaphore_signal(barrier, inc=1, device_id={"dep": other}, device_id_type=MESH)

    def zlane(zt):
        return pl.ds(pl.multiple_of(zt * LANES, LANES), LANES)

    def zero_edges(field):
        def body(zt, _):
            field[0, zt + 1] = jnp.zeros((rows, LANES), jnp.float32)
            field[xs + 1, zt + 1] = jnp.zeros((rows, LANES), jnp.float32)
            return 0

        lax.fori_loop(0, zts, body, 0)
        side = dep * (zts + 1)

        def body_z(x, _):
            field[x + 1, side] = jnp.zeros((rows, LANES), jnp.float32)
            return 0

        lax.fori_loop(0, xs, body_z, 0)

    def remote(src, dst, sem, device):
        return pltpu.make_async_remote_copy(
            src_ref=src, dst_ref=dst, send_sem=send_sem.at[sem], recv_sem=recv_sem.at[sem],
            device_id=device, device_id_type=MESH,
        )

    def to_sides(base, pieces):
        found = []
        for s, (has, device) in enumerate(sides[:len(pieces)]):
            src, dst = pieces[s]
            found.append((has, remote(src, dst, base + (s ^ 1), device)))
        return found

    def from_sides(base, pieces):
        found = []
        for s, (has, device) in enumerate(sides[:len(pieces)]):
            src, dst = pieces[s ^ 1]
            found.append((has, remote(src, dst, base + s, device)))
        return found

    def start_all(found):
        for has, copy in found:
            pl.when(has)(copy.start)

    def wait_sends(found):
        for has, copy in found:
            pl.when(has)(copy.wait_send)

    def face_pieces(field, slot):
        return [
            (field.at[1, pl.ds(1, zts)], xh.at[slot, 1]),
            (field.at[xs, pl.ds(1, zts)], xh.at[slot, 0]),
        ]

    odd = lax.rem(col, 2)
    straight = col + 1 - 2 * odd
    has_across = jnp.where(odd == 1, col < n_col - 1, col > 0)
    across = col - 1 + 2 * odd
    corner = col - 2 + 4 * odd
    passes_on = jnp.where(odd == 1, col > 1, col < n_col - 2)
    pass_to = col + 1 - 2 * odd
    half = xs // 2

    def y_copy(src, dst, send, recv, device):
        return pltpu.make_async_remote_copy(
            src_ref=src, dst_ref=dst, send_sem=send, recv_sem=recv,
            device_id={"col": device}, device_id_type=MESH,
        )

    def straight_copy(slot, k):
        x = order(k)
        return y_copy(ys.at[slot, 1 - odd, x], yh.at[slot, odd, x], y_send.at[slot, 0, k],
                      y_recv.at[slot, odd, x], straight)

    def across_copy(slot, k, part):
        x = order(k)
        if part == 0:
            return y_copy(ys.at[slot, odd, x], relay.at[slot, k // 2], y_send.at[slot, 1, k],
                          r_recv.at[slot, k // 2], corner)
        return y_copy(ys.at[slot, odd, x], yh.at[slot, 1 - odd, x], y_send.at[slot, 1, k],
                      y_recv.at[slot, 1 - odd, x], across)

    def pass_copy(slot, j):
        x = order(2 * j)
        return y_copy(relay.at[slot, j], yh.at[slot, 1 - odd, x], r_send.at[slot, j],
                      y_recv.at[slot, 1 - odd, x], pass_to)

    def pass_on(slot, j):
        @pl.when(passes_on)
        def _():
            across_copy(slot, 2 * j, 0).wait_recv()
            pass_copy(slot, j).start()

    def send_y(slot, k, part):
        @pl.when(has_across)
        def _():
            across_copy(slot, k, part).start()

        straight_copy(slot, k).start()

    def wait_y(slot, s, x):
        y_copy(ys.at[slot, s, x], yh.at[slot, s, x], y_send.at[slot, 0, 0], y_recv.at[slot, s, x],
               straight).wait_recv()

    def pack_y(field, slot, x):
        for zt in range(zts):
            for s in range(2):
                ys[slot, s, x, zt] = field[x + 1, zt + 1, pl.ds(s * (SUB - 1), 3 * rhs, stride=SUB), :]

    own_z = (1 - dep) * (zts - 1) + 1
    halo_z = (1 - dep) * (zts + 1)
    far_z = dep * (zts + 1)

    def z_copy(field, sem):
        return remote(field.at[pl.ds(1, xs), own_z], field.at[pl.ds(1, xs), far_z], sem, {"dep": other})

    waits = [sides[2][0], sides[3][0], relays[0][0], relays[1][0]]
    pl.semaphore_wait(barrier, n_row + sum(has.astype(jnp.int32) for has in waits))
    for copy in diagonal:
        copy.wait()

    def scale(j, _):
        for part in range(2):
            k = 2 * j + part
            x = order(k)
            load_copy(x).wait()
            for c in range(3):
                weight = 0.8 / diag_v[c, c, x]
                wgt[c, x] = weight
                for zt in range(zts):
                    zl = slice(zt * LANES, (zt + 1) * LANES)
                    value = weight[:, zl][None] * load_v[c, :, x, :, zl]
                    first[x + 1, zt + 1, c * rhs * SUB:(c + 1) * rhs * SUB, :] = value.reshape(rhs * SUB, LANES)
            pack_y(first, 0, x)
            send_y(0, k, part)
        return 0

    lax.fori_loop(0, half, scale, 0)
    p1 = face_pieces(first, 0)
    e1 = to_sides(0, p1)
    start_all(e1)
    z1 = z_copy(first, 4)
    z1.start()

    aggr_copy.wait()
    for x in range(xs):
        for s in range(2):
            y = s * (SUB - 1)
            agys[s, x:x + 1, :] = ag[x, y:y + 1, :]
    pa = [
        (ag.at[0], agx.at[1]), (ag.at[xs - 1], agx.at[0]),
        (agys.at[0], agy.at[1]), (agys.at[1], agy.at[0]),
    ]
    ea = to_sides(10, pa)
    start_all(ea)
    za = remote(
        ag.at[:, :, zlane((1 - dep) * (zts - 1))], agz, 14, {"dep": other}
    )
    za.start()
    zero_edges(first)
    zero_edges(second)
    zero_edges(third)
    tabs[...] = jnp.zeros_like(tabs)
    gath[row] = jnp.zeros((3 * rhs, LANES), jnp.float32)
    for copy in (*off_diagonal, coup_copy):
        copy.wait()
    z1.wait_recv()

    lane = lax.broadcasted_iota(jnp.int32, (rb, SUB, LANES), 2)
    sub = lax.broadcasted_iota(jnp.int32, (rb, SUB, LANES), 1)
    at_first, at_last = lane == 0, lane == LANES - 1
    at_top, at_bottom = sub == 0, sub == SUB - 1

    def tile_rows(c, r0):
        return slice((c * rhs + r0) * SUB, (c * rhs + r0 + rb) * SUB)

    def tile(field, x, zt, c, r0):
        return field[x, zt, tile_rows(c, r0), :].reshape(rb, SUB, LANES)

    def operate(field, x, zt, r0):
        own = [tile(field, x + 1, zt + 1, c, r0) for c in range(3)]
        zl = zlane(zt)
        total = []
        for a in range(3):
            t = diag_v[a, 0, x, :, zl][None] * own[0]
            for c in (1, 2):
                t = t + diag_v[a, c, x, :, zl][None] * own[c]
            total.append(t)
        for d in range(6):
            for c in range(3):
                if d == 0:
                    near = tile(field, x + 2, zt + 1, c, r0)
                elif d == 1:
                    near = tile(field, x, zt + 1, c, r0)
                elif d == 2:
                    near = jnp.where(at_bottom, 0.0, pltpu.roll(own[c], SUB - 1, 1))
                elif d == 3:
                    near = jnp.where(at_top, 0.0, pltpu.roll(own[c], 1, 1))
                elif d == 4:
                    near = pltpu.roll(jnp.where(at_first, tile(field, x + 1, zt + 2, c, r0), own[c]), LANES - 1, 2)
                else:
                    near = pltpu.roll(jnp.where(at_last, tile(field, x + 1, zt, c, r0), own[c]), 1, 2)
                for a in range(3):
                    total[a] = total[a] - coup[d, a, c, x, :, zl][None] * near
        return own, total

    def sweep(body, slot=None):
        def run(i, _):
            x, zt = i // zts, i % zts
            for r0 in range(0, rhs, rb):
                body(x, zt, r0)
            return 0

        if slot is None:
            lax.fori_loop(0, xs * zts, run, 0)
            return

        def quarter(j, _):
            lax.fori_loop(2 * zts * j, 2 * zts * (j + 1), run, 0)
            pass_on(slot, j)
            return 0

        lax.fori_loop(0, half, quarter, 0)

    def smooth(x, zt, r0):
        own, total = operate(first, x, zt, r0)
        zl = zlane(zt)
        for a in range(3):
            value = own[a] + wgt[a, x, :, zl][None] * (load_v[a, r0:r0 + rb, x, :, zl] - total[a])
            second[x + 1, zt + 1, tile_rows(a, r0), :] = value.reshape(rb * SUB, LANES)

    sweep(smooth, 0)

    def fix_x(field, off, s, slot, weighted):
        x = s * (xs - 1)
        d = 1 - s

        def body(zt, _):
            zl = zlane(zt)
            for r0 in range(0, rhs, rb):
                near = [xh[slot, s, zt, tile_rows(c, r0), :].reshape(rb, SUB, LANES) for c in range(3)]
                for a in range(3):
                    t = coup[d, a, 0, x, :, zl][None] * near[0]
                    for c in (1, 2):
                        t = t + coup[d, a, c, x, :, zl][None] * near[c]
                    t = t.reshape(rb * SUB, LANES)
                    if weighted:
                        t = (wgt[a, x, :, zl][None] * t.reshape(rb, SUB, LANES)).reshape(rb * SUB, LANES)
                        field[x + off, zt + off, tile_rows(a, r0), :] += t
                    else:
                        field[x + off, zt + off, tile_rows(a, r0), :] += t
            return 0

        lax.fori_loop(0, zts, body, 0)

    def fix_y(field, off, s, slot, weighted, x):
        y = s * (SUB - 1)
        d = 3 - s
        for zt in range(zts):
            zl = slice(zt * LANES, (zt + 1) * LANES)
            near = [yh[slot, s, x, zt, c * rhs:(c + 1) * rhs, :] for c in range(3)]
            for a in range(3):
                t = coup[d, a, 0, x, y:y + 1, zl] * near[0]
                for c in (1, 2):
                    t = t + coup[d, a, c, x, y:y + 1, zl] * near[c]
                if weighted:
                    t = wgt[a, x, y:y + 1, zl] * t
                at = pl.ds(a * rhs * SUB + y, rhs, stride=SUB)
                field[x + off, zt + off, at, :] = field[x + off, zt + off, at, :] + t

    def fix_x_arrived(arrivals, field, off, slot, weighted):
        for s, (has, copy) in enumerate(arrivals):
            @pl.when(has)
            def _():
                copy.wait_recv()
                fix_x(field, off, s, slot, weighted)

    def fix_y_arrived(field, off, slot, weighted, x):
        for s in range(2):
            @pl.when(sides[2 + s][0])
            def _():
                wait_y(slot, s, x)
                fix_y(field, off, s, slot, weighted, x)

    def renew(j, _):
        @pl.when(j == half - 1)
        def _():
            fix_x_arrived(from_sides(0, p1), second, 1, 0, True)

        for part in range(2):
            k = 2 * j + part
            x = order(k)
            fix_y_arrived(second, 1, 0, True, x)
            pack_y(second, 1, x)
            send_y(1, k, part)
        return 0

    lax.fori_loop(0, half, renew, 0)
    p2 = face_pieces(second, 1)
    e2 = to_sides(5, p2)
    start_all(e2)
    z2 = z_copy(second, 9)
    z2.start()
    z2.wait_recv()

    def defect(x, zt, r0):
        own, total = operate(second, x, zt, r0)
        zl = zlane(zt)
        for a in range(3):
            value = load_v[a, r0:r0 + rb, x, :, zl] - total[a]
            resid[x, zt, tile_rows(a, r0), :] = value.reshape(rb * SUB, LANES)

    sweep(defect, 1)

    number = lax.broadcasted_iota(jnp.int32, (agg, zts * LANES), 0)

    def restrict(x, total, lines):
        for y in lines:
            value = jnp.concatenate(
                [resid[x, zt, pl.ds(y, 3 * rhs, stride=SUB), :] for zt in range(zts)], axis=1
            )
            high = value.astype(jnp.bfloat16).astype(jnp.float32)
            both = jnp.concatenate([high, value - high], axis=0).astype(jnp.bfloat16)
            member = (ag[x, y:y + 1, :] == number).astype(jnp.float32).astype(jnp.bfloat16)
            total = total + lax.dot_general(
                both, member, (((1,), (1,)), ((), ())), preferred_element_type=jnp.float32
            )
        return total

    inner = range(1, SUB - 1)
    sums = lax.fori_loop(
        1, xs - 1, lambda x, total: restrict(x, total, inner), jnp.zeros((6 * rhs, agg), jnp.float32)
    )

    def finish(k, total):
        x = order(k)
        fix_y_arrived(resid, 0, 1, False, x)
        return restrict(x, total, (0, SUB - 1))

    sums = lax.fori_loop(0, xs - 2, finish, sums)
    fix_x_arrived(from_sides(5, p2), resid, 0, 1, False)

    def finish_edge(k, total):
        x = order(k)
        total = restrict(x, total, inner)
        fix_y_arrived(resid, 0, 1, False, x)
        return restrict(x, total, (0, SUB - 1))

    sums = lax.fori_loop(xs - 2, xs, finish_edge, sums)
    inv_copy.wait()
    gath[row, :, 0:agg] = sums[:3 * rhs] + sums[3 * rhs:]
    gathers = []
    for step in range(1, n_row):
        copy = pltpu.make_async_remote_copy(
            src_ref=gath.at[row], dst_ref=gath.at[row], send_sem=g_send.at[step - 1], recv_sem=g_recv.at[step - 1],
            device_id={"row": lax.rem(row + step, n_row)}, device_id_type=MESH,
        )
        copy.start()
        gathers.append(copy)
    for step in range(1, n_row):
        source = lax.rem(row + n_row - step, n_row)
        pltpu.make_async_remote_copy(
            src_ref=gath.at[source], dst_ref=gath.at[source], send_sem=g_send.at[step - 1],
            recv_sem=g_recv.at[step - 1], device_id={"row": source}, device_id_type=MESH,
        ).wait_recv()
    vector = jnp.concatenate(
        [gath[i, c * rhs:(c + 1) * rhs, 0:agg] for i in range(n_row) for c in range(3)], axis=1
    )
    solved = lax.dot_general(
        vector, inv[...], (((1,), (1,)), ((), ())), precision=lax.Precision.HIGHEST,
        preferred_element_type=jnp.float32,
    )
    for c in range(3):
        tabs[0, c * rhs:(c + 1) * rhs, 0:agg] = solved[:, c * agg:(c + 1) * agg]
    pt = [(tabs.at[0], tabs.at[1 + (s ^ 1)]) for s in range(4)]
    et = to_sides(15, pt)
    start_all(et)
    zt_copy = remote(tabs.at[0], tabs.at[5], 19, {"dep": other})
    zt_copy.start()

    def look(table, index):
        return jnp.take_along_axis(table, index, axis=1, mode="promise_in_bounds")

    def spread(i, _):
        x, zt = i // zts, i % zts
        index = ag[x, :, zlane(zt)]
        for k in range(3 * rhs):
            table = jnp.broadcast_to(tabs[0, k:k + 1, :], (SUB, LANES))
            third[x + 1, zt + 1, k * SUB:(k + 1) * SUB, :] = look(table, index)
        return 0

    lax.fori_loop(0, xs * zts, spread, 0)
    zt_copy.wait_recv()
    za.wait_recv()

    def spread_z(x, _):
        index = agz[x]
        for k in range(3 * rhs):
            table = jnp.broadcast_to(tabs[5, k:k + 1, :], (SUB, LANES))
            third[x + 1, halo_z, k * SUB:(k + 1) * SUB, :] = look(table, index)
        return 0

    lax.fori_loop(0, xs, spread_z, 0)

    def final(x, zt, r0):
        own, total = operate(third, x, zt, r0)
        zl = zlane(zt)
        for a in range(3):
            left = resid[x, zt, tile_rows(a, r0), :].reshape(rb, SUB, LANES) - total[a]
            value = tile(second, x + 1, zt + 1, a, r0) + own[a] + wgt[a, x, :, zl][None] * left
            out_v[x, zt, tile_rows(a, r0), :] = value.reshape(rb * SUB, LANES)

    sweep(final)

    arrived_t, arrived_a = from_sides(15, pt), from_sides(10, pa)
    for s in range(4):
        has = sides[s][0]

        @pl.when(has)
        def _():
            arrived_t[s][1].wait_recv()
            arrived_a[s][1].wait_recv()
            if s < 2:
                def body(zt, _):
                    index = agx[s, :, zlane(zt)]
                    for k in range(3 * rhs):
                        table = jnp.broadcast_to(tabs[1 + s, k:k + 1, :], (SUB, LANES))
                        xh[2, s, zt, k * SUB:(k + 1) * SUB, :] = look(table, index)
                    return 0

                lax.fori_loop(0, zts, body, 0)
                fix_x(out_v, 0, s, 2, True)
            else:
                for x in range(xs):
                    for zt in range(zts):
                        zl = slice(zt * LANES, (zt + 1) * LANES)
                        index = jnp.broadcast_to(agy[s - 2, x:x + 1, zl], (SUB, LANES))
                        for c in range(3):
                            yh[2, s - 2, x, zt, c * rhs:(c + 1) * rhs, :] = look(
                                tabs[1 + s, c * rhs:(c + 1) * rhs, :], index
                            )

                def body_y(x, _):
                    fix_y(out_v, 0, s - 2, 2, True, x)
                    return 0

                lax.fori_loop(0, xs, body_y, 0)

    for found in (e1, e2, ea, et):
        wait_sends(found)
    for copy in (z1, z2, za, zt_copy, *gathers):
        copy.wait_send()

    def wait_y_sends(j, _):
        for slot in range(2):
            for part in range(2):
                straight_copy(slot, 2 * j + part).wait_send()

                @pl.when(has_across)
                def _():
                    across_copy(slot, 2 * j + part, part).wait_send()

            @pl.when(passes_on)
            def _():
                pass_copy(slot, j).wait_send()
        return 0

    lax.fori_loop(0, half, wait_y_sends, 0)


def deliver(tiles, out_h, sem):
    xs, zts = tiles.shape[0], tiles.shape[1]
    _, rhs, _, sub, _ = out_h.shape
    copies = []
    for x in range(xs):
        for zt in range(zts):
            copies.append(pltpu.make_async_copy(
                tiles.at[x, zt].reshape(3, rhs, sub, LANES),
                out_h.at[:, :, x, :, pl.ds(zt * LANES, LANES)],
                sem.at[x * zts + zt],
            ))
    for copy in copies:
        copy.start()
    for copy in copies:
        copy.wait()


def on_device(n_row, n_col, load, diagonal_block, coupling, aggregates, coarse_inverse):
    _, rhs, xs, sub, depth = load.shape
    zts = depth // LANES
    ncg = coarse_inverse.shape[-1]
    agg = ncg // n_row // 3
    rows = 3 * rhs * sub
    f32 = jnp.float32
    dma = pltpu.SemaphoreType.DMA
    field = pltpu.VMEM((xs + 2, zts + 2, rows, LANES), f32)
    block = pltpu.VMEM((xs, zts, rows, LANES), f32)
    tiles = pl.pallas_call(
        functools.partial(kernel, n_row, n_col, agg),
        out_shape=pltpu.VMEM((xs, zts, rows, LANES), f32),
        in_specs=[pl.BlockSpec(memory_space=pl.ANY)] * 5,
        out_specs=pl.BlockSpec(memory_space=pltpu.VMEM),
        scratch_shapes=[
            pltpu.VMEM(load.shape, f32),
            pltpu.VMEM(diagonal_block.shape, f32),
            pltpu.VMEM(coupling.shape, f32),
            pltpu.VMEM(aggregates.shape, jnp.int32),
            pltpu.VMEM((3 * agg, ncg), f32),
            pltpu.VMEM((3, xs, sub, depth), f32),
            field, field, block, field,
            pltpu.VMEM((3, 2, zts, rows, LANES), f32),
            pltpu.VMEM((3, 2, xs, zts, 3 * rhs, LANES), f32),
            pltpu.VMEM((2, 2, xs, zts, 3 * rhs, LANES), f32),
            pltpu.VMEM((2, xs // 2, zts, 3 * rhs, LANES), f32),
            pltpu.VMEM((2, sub, depth), jnp.int32),
            pltpu.VMEM((2, xs, depth), jnp.int32),
            pltpu.VMEM((2, xs, depth), jnp.int32),
            pltpu.VMEM((xs, sub, LANES), jnp.int32),
            pltpu.VMEM((n_row, 3 * rhs, LANES), f32),
            pltpu.VMEM((6, 3 * rhs, LANES), f32),
            dma((12,)),
            dma((xs,)),
            dma((20,)),
            dma((20,)),
            dma((2, 2, xs)),
            dma((2, 2, xs)),
            dma((2, xs // 2)),
            dma((2, xs // 2)),
            dma((n_row - 1,)),
            dma((n_row - 1,)),
        ],
        compiler_params=pltpu.CompilerParams(
            collective_id=0, has_side_effects=True, vmem_limit_bytes=52 * 2**20
        ),
    )(load, diagonal_block, coupling, aggregates, coarse_inverse)
    return pl.pallas_call(
        deliver,
        out_shape=jax.ShapeDtypeStruct(load.shape, f32),
        in_specs=[pl.BlockSpec(memory_space=pl.ANY)],
        out_specs=pl.BlockSpec(memory_space=pl.ANY),
        scratch_shapes=[dma((xs * zts,))],
        compiler_params=pltpu.CompilerParams(vmem_limit_bytes=2**20),
    )(tiles)


def solution(mesh):
    in_specs = (
        P(None, None, "row", "col", "dep"),
        P(None, None, "row", "col", "dep"),
        P(None, None, None, "row", "col", "dep"),
        P("row", "col", "dep"),
        P("col", "dep", None, None),
    )
    out_specs = P(None, None, "row", "col", "dep")
    return jax.shard_map(
        functools.partial(on_device, mesh.shape["row"], mesh.shape["col"]),
        mesh=mesh, in_specs=in_specs, out_specs=out_specs, check_vma=False,
    )
```

```python
import functools

import jax
import jax.numpy as jnp
from jax import lax
from jax.experimental import pallas as pl
from jax.experimental.pallas import tpu as pltpu
from jax.sharding import PartitionSpec as P

LANES = 128
SUB = 8
MESH = pl.DeviceIdType.MESH


def kernel(
    n_row, n_col, agg,
    load_h, diag_h, coup_h, aggr_h, inv_h, out_v,
    load_v, diag_v, coup, ag, inv, inv_parts, wgt, first, second, resid, third,
    xh, yh, ys, relay, agx, agy, agys, agz, gath, tabs,
    in_sem, load_sem, send_sem, recv_sem, y_send, y_recv, r_send, r_recv, g_send, g_recv,
):
    rhs, xs = load_v.shape[1], load_v.shape[2]
    zts = load_v.shape[4] // LANES
    rows = 3 * rhs * SUB
    rb = 4
    row, col, dep = lax.axis_index("row"), lax.axis_index("col"), lax.axis_index("dep")
    other = 1 - dep
    own_rows = 3 * agg

    def order(k):
        return jnp.where(k < xs - 2, k + 1, jnp.where(k == xs - 2, 0, xs - 1))

    def load_copy(x):
        return pltpu.make_async_copy(load_h.at[:, :, x], load_v.at[:, :, x], load_sem.at[x])

    diagonal = [
        pltpu.make_async_copy(diag_h.at[c, c], diag_v.at[c, c], in_sem.at[3 * c + c]) for c in range(3)
    ]
    off_diagonal = [
        pltpu.make_async_copy(diag_h.at[a, c], diag_v.at[a, c], in_sem.at[3 * a + c])
        for a in range(3) for c in range(3) if a != c
    ]
    aggr_copy = pltpu.make_async_copy(aggr_h, ag, in_sem.at[9])
    coup_copy = pltpu.make_async_copy(coup_h, coup, in_sem.at[10])
    inv_copy = pltpu.make_async_copy(
        inv_h.at[0, 0, pl.ds(pl.multiple_of(row * own_rows, SUB), own_rows), :], inv, in_sem.at[11]
    )
    for copy in diagonal:
        copy.start()
    for x in [*range(1, xs - 1), 0, xs - 1]:
        load_copy(x).start()
    for copy in (aggr_copy, *off_diagonal, coup_copy, inv_copy):
        copy.start()

    sides = [
        (row > 0, {"row": row - 1}),
        (row < n_row - 1, {"row": row + 1}),
        (col > 0, {"col": col - 1}),
        (col < n_col - 1, {"col": col + 1}),
    ]
    barrier = pltpu.get_barrier_semaphore()
    for step in range(1, n_row):
        pl.semaphore_signal(barrier, inc=1, device_id={"row": lax.rem(row + step, n_row)}, device_id_type=MESH)
    for has, device in sides[2:]:
        @pl.when(has)
        def _():
            pl.semaphore_signal(barrier, inc=1, device_id=device, device_id_type=MESH)
    relays = [(col > 1, {"col": col - 2}), (col < n_col - 2, {"col": col + 2})]
    for has, device in relays:
        @pl.when(has)
        def _():
            pl.semaphore_signal(barrier, inc=1, device_id=device, device_id_type=MESH)
    pl.semaphore_signal(barrier, inc=1, device_id={"dep": other}, device_id_type=MESH)

    def zlane(zt):
        return pl.ds(pl.multiple_of(zt * LANES, LANES), LANES)

    def zero_edges(field):
        def body(zt, _):
            field[0, zt + 1] = jnp.zeros((rows, LANES), jnp.float32)
            field[xs + 1, zt + 1] = jnp.zeros((rows, LANES), jnp.float32)
            return 0

        lax.fori_loop(0, zts, body, 0)
        side = dep * (zts + 1)

        def body_z(x, _):
            field[x + 1, side] = jnp.zeros((rows, LANES), jnp.float32)
            return 0

        lax.fori_loop(0, xs, body_z, 0)

    def remote(src, dst, sem, device):
        return pltpu.make_async_remote_copy(
            src_ref=src, dst_ref=dst, send_sem=send_sem.at[sem], recv_sem=recv_sem.at[sem],
            device_id=device, device_id_type=MESH,
        )

    def to_sides(base, pieces):
        found = []
        for s, (has, device) in enumerate(sides[:len(pieces)]):
            src, dst = pieces[s]
            found.append((has, remote(src, dst, base + (s ^ 1), device)))
        return found

    def from_sides(base, pieces):
        found = []
        for s, (has, device) in enumerate(sides[:len(pieces)]):
            src, dst = pieces[s ^ 1]
            found.append((has, remote(src, dst, base + s, device)))
        return found

    def start_all(found):
        for has, copy in found:
            pl.when(has)(copy.start)

    def wait_sends(found):
        for has, copy in found:
            pl.when(has)(copy.wait_send)

    def face_pieces(field, slot):
        return [
            (field.at[1, pl.ds(1, zts)], xh.at[slot, 1]),
            (field.at[xs, pl.ds(1, zts)], xh.at[slot, 0]),
        ]

    odd = lax.rem(col, 2)
    straight = col + 1 - 2 * odd
    has_across = jnp.where(odd == 1, col < n_col - 1, col > 0)
    across = col - 1 + 2 * odd
    corner = col - 2 + 4 * odd
    passes_on = jnp.where(odd == 1, col > 1, col < n_col - 2)
    pass_to = col + 1 - 2 * odd
    half = xs // 2

    def y_copy(src, dst, send, recv, device):
        return pltpu.make_async_remote_copy(
            src_ref=src, dst_ref=dst, send_sem=send, recv_sem=recv,
            device_id={"col": device}, device_id_type=MESH,
        )

    def straight_copy(slot, k):
        x = order(k)
        return y_copy(ys.at[slot, 1 - odd, x], yh.at[slot, odd, x], y_send.at[slot, 0, k],
                      y_recv.at[slot, odd, x], straight)

    def across_copy(slot, k, part):
        x = order(k)
        if part == 0:
            return y_copy(ys.at[slot, odd, x], relay.at[slot, k // 2], y_send.at[slot, 1, k],
                          r_recv.at[slot, k // 2], corner)
        return y_copy(ys.at[slot, odd, x], yh.at[slot, 1 - odd, x], y_send.at[slot, 1, k],
                      y_recv.at[slot, 1 - odd, x], across)

    def pass_copy(slot, j):
        x = order(2 * j)
        return y_copy(relay.at[slot, j], yh.at[slot, 1 - odd, x], r_send.at[slot, j],
                      y_recv.at[slot, 1 - odd, x], pass_to)

    def pass_on(slot, j):
        @pl.when(passes_on)
        def _():
            across_copy(slot, 2 * j, 0).wait_recv()
            pass_copy(slot, j).start()

    def send_y(slot, k, part):
        @pl.when(has_across)
        def _():
            across_copy(slot, k, part).start()

        straight_copy(slot, k).start()

    def wait_y(slot, s, x):
        y_copy(ys.at[slot, s, x], yh.at[slot, s, x], y_send.at[slot, 0, 0], y_recv.at[slot, s, x],
               straight).wait_recv()

    def pack_y(field, slot, x):
        for zt in range(zts):
            for s in range(2):
                ys[slot, s, x, zt] = field[x + 1, zt + 1, pl.ds(s * (SUB - 1), 3 * rhs, stride=SUB), :]

    own_z = (1 - dep) * (zts - 1) + 1
    halo_z = (1 - dep) * (zts + 1)
    far_z = dep * (zts + 1)

    def z_copy(field, sem):
        return remote(field.at[pl.ds(1, xs), own_z], field.at[pl.ds(1, xs), far_z], sem, {"dep": other})

    waits = [sides[2][0], sides[3][0], relays[0][0], relays[1][0]]
    pl.semaphore_wait(barrier, n_row + sum(has.astype(jnp.int32) for has in waits))
    for copy in diagonal:
        copy.wait()

    def scale(j, _):
        for part in range(2):
            k = 2 * j + part
            x = order(k)
            load_copy(x).wait()
            for c in range(3):
                weight = 0.8 / diag_v[c, c, x]
                wgt[c, x] = weight
                for zt in range(zts):
                    zl = slice(zt * LANES, (zt + 1) * LANES)
                    value = weight[:, zl][None] * load_v[c, :, x, :, zl]
                    first[x + 1, zt + 1, c * rhs * SUB:(c + 1) * rhs * SUB, :] = value.reshape(rhs * SUB, LANES)
            pack_y(first, 0, x)
            send_y(0, k, part)
        return 0

    lax.fori_loop(0, half, scale, 0)
    p1 = face_pieces(first, 0)
    e1 = to_sides(0, p1)
    start_all(e1)
    z1 = z_copy(first, 4)
    z1.start()

    aggr_copy.wait()
    for x in range(xs):
        for s in range(2):
            y = s * (SUB - 1)
            agys[s, x:x + 1, :] = ag[x, y:y + 1, :]
    pa = [
        (ag.at[0], agx.at[1]), (ag.at[xs - 1], agx.at[0]),
        (agys.at[0], agy.at[1]), (agys.at[1], agy.at[0]),
    ]
    ea = to_sides(10, pa)
    start_all(ea)
    za = remote(
        ag.at[:, :, zlane((1 - dep) * (zts - 1))], agz, 14, {"dep": other}
    )
    za.start()
    zero_edges(first)
    zero_edges(second)
    zero_edges(third)
    tabs[...] = jnp.zeros_like(tabs)
    gath[row] = jnp.zeros((3 * rhs, LANES), jnp.float32)
    for copy in (*off_diagonal, coup_copy):
        copy.wait()
    z1.wait_recv()

    lane = lax.broadcasted_iota(jnp.int32, (rb, SUB, LANES), 2)
    sub = lax.broadcasted_iota(jnp.int32, (rb, SUB, LANES), 1)
    at_first, at_last = lane == 0, lane == LANES - 1
    at_top, at_bottom = sub == 0, sub == SUB - 1

    def tile_rows(c, r0):
        return slice((c * rhs + r0) * SUB, (c * rhs + r0 + rb) * SUB)

    def tile(field, x, zt, c, r0):
        return field[x, zt, tile_rows(c, r0), :].reshape(rb, SUB, LANES)

    def operate(field, x, zt, r0):
        own = [tile(field, x + 1, zt + 1, c, r0) for c in range(3)]
        zl = zlane(zt)
        total = []
        for a in range(3):
            t = diag_v[a, 0, x, :, zl][None] * own[0]
            for c in (1, 2):
                t = t + diag_v[a, c, x, :, zl][None] * own[c]
            total.append(t)
        for d in range(6):
            for c in range(3):
                if d == 0:
                    near = tile(field, x + 2, zt + 1, c, r0)
                elif d == 1:
                    near = tile(field, x, zt + 1, c, r0)
                elif d == 2:
                    near = jnp.where(at_bottom, 0.0, pltpu.roll(own[c], SUB - 1, 1))
                elif d == 3:
                    near = jnp.where(at_top, 0.0, pltpu.roll(own[c], 1, 1))
                elif d == 4:
                    near = pltpu.roll(jnp.where(at_first, tile(field, x + 1, zt + 2, c, r0), own[c]), LANES - 1, 2)
                else:
                    near = pltpu.roll(jnp.where(at_last, tile(field, x + 1, zt, c, r0), own[c]), 1, 2)
                for a in range(3):
                    total[a] = total[a] - coup[d, a, c, x, :, zl][None] * near
        return own, total

    def sweep(body, slot=None):
        def run(i, _):
            x, zt = i // zts, i % zts
            for r0 in range(0, rhs, rb):
                body(x, zt, r0)
            return 0

        if slot is None:
            lax.fori_loop(0, xs * zts, run, 0)
            return

        def quarter(j, _):
            lax.fori_loop(2 * zts * j, 2 * zts * (j + 1), run, 0)
            if slot == 0:
                pass_on(slot, j)
            else:
                pl.when(j == 0)(lambda: pass_on(slot, half - 1))
            return 0

        lax.fori_loop(0, half, quarter, 0)

    def smooth(x, zt, r0):
        own, total = operate(first, x, zt, r0)
        zl = zlane(zt)
        for a in range(3):
            value = own[a] + wgt[a, x, :, zl][None] * (load_v[a, r0:r0 + rb, x, :, zl] - total[a])
            second[x + 1, zt + 1, tile_rows(a, r0), :] = value.reshape(rb * SUB, LANES)

    sweep(smooth, 0)

    def fix_x(field, off, s, slot, weighted):
        x = s * (xs - 1)
        d = 1 - s

        def body(zt, _):
            zl = zlane(zt)
            for r0 in range(0, rhs, rb):
                near = [xh[slot, s, zt, tile_rows(c, r0), :].reshape(rb, SUB, LANES) for c in range(3)]
                for a in range(3):
                    t = coup[d, a, 0, x, :, zl][None] * near[0]
                    for c in (1, 2):
                        t = t + coup[d, a, c, x, :, zl][None] * near[c]
                    t = t.reshape(rb * SUB, LANES)
                    if weighted:
                        t = (wgt[a, x, :, zl][None] * t.reshape(rb, SUB, LANES)).reshape(rb * SUB, LANES)
                        field[x + off, zt + off, tile_rows(a, r0), :] += t
                    else:
                        field[x + off, zt + off, tile_rows(a, r0), :] += t
            return 0

        lax.fori_loop(0, zts, body, 0)

    def fix_y(field, off, s, slot, weighted, x):
        y = s * (SUB - 1)
        d = 3 - s
        for zt in range(zts):
            zl = slice(zt * LANES, (zt + 1) * LANES)
            near = [yh[slot, s, x, zt, c * rhs:(c + 1) * rhs, :] for c in range(3)]
            for a in range(3):
                t = coup[d, a, 0, x, y:y + 1, zl] * near[0]
                for c in (1, 2):
                    t = t + coup[d, a, c, x, y:y + 1, zl] * near[c]
                if weighted:
                    t = wgt[a, x, y:y + 1, zl] * t
                at = pl.ds(a * rhs * SUB + y, rhs, stride=SUB)
                field[x + off, zt + off, at, :] = field[x + off, zt + off, at, :] + t

    def fix_x_arrived(arrivals, field, off, slot, weighted):
        for s, (has, copy) in enumerate(arrivals):
            @pl.when(has)
            def _():
                copy.wait_recv()
                fix_x(field, off, s, slot, weighted)

    def fix_y_arrived(field, off, slot, weighted, x):
        for s in range(2):
            @pl.when(sides[2 + s][0])
            def _():
                wait_y(slot, s, x)
                fix_y(field, off, s, slot, weighted, x)

    def renew(j, _):
        @pl.when(j == half - 1)
        def _():
            fix_x_arrived(from_sides(0, p1), second, 1, 0, True)

        for part in range(2):
            k = 2 * j + part
            x = order(k)
            fix_y_arrived(second, 1, 0, True, x)
            pack_y(second, 1, x)
            send_y(1, k, part)

        @pl.when(j > 0)
        def _():
            pass_on(1, j - 1)

        return 0

    lax.fori_loop(0, half, renew, 0)
    p2 = face_pieces(second, 1)
    e2 = to_sides(5, p2)
    start_all(e2)
    z2 = z_copy(second, 9)
    z2.start()
    z2.wait_recv()

    def defect(x, zt, r0):
        own, total = operate(second, x, zt, r0)
        zl = zlane(zt)
        for a in range(3):
            value = load_v[a, r0:r0 + rb, x, :, zl] - total[a]
            resid[x, zt, tile_rows(a, r0), :] = value.reshape(rb * SUB, LANES)

    sweep(defect, 1)

    number = lax.broadcasted_iota(jnp.int32, (agg, zts * LANES), 0)

    def restrict(x, total, lines):
        for y in lines:
            value = jnp.concatenate(
                [resid[x, zt, pl.ds(y, 3 * rhs, stride=SUB), :] for zt in range(zts)], axis=1
            )
            high = value.astype(jnp.bfloat16).astype(jnp.float32)
            both = jnp.concatenate([high, value - high], axis=0).astype(jnp.bfloat16)
            member = (ag[x, y:y + 1, :] == number).astype(jnp.float32).astype(jnp.bfloat16)
            total = total + lax.dot_general(
                both, member, (((1,), (1,)), ((), ())), preferred_element_type=jnp.float32
            )
        return total

    inv_copy.wait()
    inv_parts[0] = inv[...].astype(jnp.bfloat16)
    inv_parts[1] = (inv[...] - inv_parts[0].astype(jnp.float32)).astype(jnp.bfloat16)
    inner = range(1, SUB - 1)
    sums = lax.fori_loop(
        1, xs - 1, lambda x, total: restrict(x, total, inner), jnp.zeros((6 * rhs, agg), jnp.float32)
    )

    def finish(k, total):
        x = order(k)
        fix_y_arrived(resid, 0, 1, False, x)
        return restrict(x, total, (0, SUB - 1))

    sums = lax.fori_loop(0, xs - 2, finish, sums)
    fix_x_arrived(from_sides(5, p2), resid, 0, 1, False)

    def finish_edge(k, total):
        x = order(k)
        total = restrict(x, total, inner)
        fix_y_arrived(resid, 0, 1, False, x)
        return restrict(x, total, (0, SUB - 1))

    sums = lax.fori_loop(xs - 2, xs, finish_edge, sums)
    gath[row, :, 0:agg] = sums[:3 * rhs] + sums[3 * rhs:]
    gathers = []
    for step in range(1, n_row):
        copy = pltpu.make_async_remote_copy(
            src_ref=gath.at[row], dst_ref=gath.at[row], send_sem=g_send.at[step - 1], recv_sem=g_recv.at[step - 1],
            device_id={"row": lax.rem(row + step, n_row)}, device_id_type=MESH,
        )
        copy.start()
        gathers.append(copy)
    for step in range(1, n_row):
        source = lax.rem(row + n_row - step, n_row)
        pltpu.make_async_remote_copy(
            src_ref=gath.at[source], dst_ref=gath.at[source], send_sem=g_send.at[step - 1],
            recv_sem=g_recv.at[step - 1], device_id={"row": source}, device_id_type=MESH,
        ).wait_recv()
    vector = jnp.concatenate(
        [gath[i, c * rhs:(c + 1) * rhs, 0:agg] for i in range(n_row) for c in range(3)], axis=1
    )
    high = vector.astype(jnp.bfloat16).astype(jnp.float32)
    both = jnp.concatenate([high, vector - high], axis=0).astype(jnp.bfloat16)
    products = sum(
        lax.dot_general(both, inv_parts[i], (((1,), (1,)), ((), ())), preferred_element_type=jnp.float32)
        for i in (1, 0)
    )
    solved = products[rhs:] + products[:rhs]
    for c in range(3):
        tabs[0, c * rhs:(c + 1) * rhs, 0:agg] = solved[:, c * agg:(c + 1) * agg]
    pt = [(tabs.at[0], tabs.at[1 + (s ^ 1)]) for s in range(4)]
    et = to_sides(15, pt)
    start_all(et)
    zt_copy = remote(tabs.at[0], tabs.at[5], 19, {"dep": other})
    zt_copy.start()

    def look(table, index):
        return jnp.take_along_axis(table, index, axis=1, mode="promise_in_bounds")

    def spread(i, _):
        x, zt = i // zts, i % zts
        index = ag[x, :, zlane(zt)]
        for k in range(3 * rhs):
            table = jnp.broadcast_to(tabs[0, k:k + 1, :], (SUB, LANES))
            third[x + 1, zt + 1, k * SUB:(k + 1) * SUB, :] = look(table, index)
        return 0

    lax.fori_loop(0, xs * zts, spread, 0)
    zt_copy.wait_recv()
    za.wait_recv()

    def spread_z(x, _):
        index = agz[x]
        for k in range(3 * rhs):
            table = jnp.broadcast_to(tabs[5, k:k + 1, :], (SUB, LANES))
            third[x + 1, halo_z, k * SUB:(k + 1) * SUB, :] = look(table, index)
        return 0

    lax.fori_loop(0, xs, spread_z, 0)

    def final(x, zt, r0):
        own, total = operate(third, x, zt, r0)
        zl = zlane(zt)
        for a in range(3):
            left = resid[x, zt, tile_rows(a, r0), :].reshape(rb, SUB, LANES) - total[a]
            value = tile(second, x + 1, zt + 1, a, r0) + own[a] + wgt[a, x, :, zl][None] * left
            out_v[x, zt, tile_rows(a, r0), :] = value.reshape(rb * SUB, LANES)

    arrived_t, arrived_a = from_sides(15, pt), from_sides(10, pa)
    for s in range(2):
        @pl.when(sides[s][0])
        def _():
            arrived_t[s][1].wait_recv()
            arrived_a[s][1].wait_recv()

            def body(zt, _):
                index = agx[s, :, zlane(zt)]
                for k in range(3 * rhs):
                    table = jnp.broadcast_to(tabs[1 + s, k:k + 1, :], (SUB, LANES))
                    third[s * (xs + 1), zt + 1, k * SUB:(k + 1) * SUB, :] = look(table, index)
                return 0

            lax.fori_loop(0, zts, body, 0)

    sweep(final)

    for s in range(2, 4):
        @pl.when(sides[s][0])
        def _():
            arrived_t[s][1].wait_recv()
            arrived_a[s][1].wait_recv()
            for x in range(xs):
                for zt in range(zts):
                    zl = slice(zt * LANES, (zt + 1) * LANES)
                    index = jnp.broadcast_to(agy[s - 2, x:x + 1, zl], (SUB, LANES))
                    for c in range(3):
                        yh[2, s - 2, x, zt, c * rhs:(c + 1) * rhs, :] = look(
                            tabs[1 + s, c * rhs:(c + 1) * rhs, :], index
                        )

            def body_y(x, _):
                fix_y(out_v, 0, s - 2, 2, True, x)
                return 0

            lax.fori_loop(0, xs, body_y, 0)

    for found in (e1, e2, ea, et):
        wait_sends(found)
    for copy in (z1, z2, za, zt_copy, *gathers):
        copy.wait_send()

    def wait_y_sends(j, _):
        for slot in range(2):
            for part in range(2):
                straight_copy(slot, 2 * j + part).wait_send()

                @pl.when(has_across)
                def _():
                    across_copy(slot, 2 * j + part, part).wait_send()

            @pl.when(passes_on)
            def _():
                pass_copy(slot, j).wait_send()
        return 0

    lax.fori_loop(0, half, wait_y_sends, 0)


def deliver(tiles, out_h, sem):
    xs, zts = tiles.shape[0], tiles.shape[1]
    _, rhs, _, sub, _ = out_h.shape
    copies = []
    for x in range(xs):
        for zt in range(zts):
            copies.append(pltpu.make_async_copy(
                tiles.at[x, zt].reshape(3, rhs, sub, LANES),
                out_h.at[:, :, x, :, pl.ds(zt * LANES, LANES)],
                sem.at[x * zts + zt],
            ))
    for copy in copies:
        copy.start()
    for copy in copies:
        copy.wait()


def on_device(n_row, n_col, load, diagonal_block, coupling, aggregates, coarse_inverse):
    _, rhs, xs, sub, depth = load.shape
    zts = depth // LANES
    ncg = coarse_inverse.shape[-1]
    agg = ncg // n_row // 3
    rows = 3 * rhs * sub
    f32 = jnp.float32
    dma = pltpu.SemaphoreType.DMA
    field = pltpu.VMEM((xs + 2, zts + 2, rows, LANES), f32)
    block = pltpu.VMEM((xs, zts, rows, LANES), f32)
    tiles = pl.pallas_call(
        functools.partial(kernel, n_row, n_col, agg),
        out_shape=pltpu.VMEM((xs, zts, rows, LANES), f32),
        in_specs=[pl.BlockSpec(memory_space=pl.ANY)] * 5,
        out_specs=pl.BlockSpec(memory_space=pltpu.VMEM),
        scratch_shapes=[
            pltpu.VMEM(load.shape, f32),
            pltpu.VMEM(diagonal_block.shape, f32),
            pltpu.VMEM(coupling.shape, f32),
            pltpu.VMEM(aggregates.shape, jnp.int32),
            pltpu.VMEM((3 * agg, ncg), f32),
            pltpu.VMEM((2, 3 * agg, ncg), jnp.bfloat16),
            pltpu.VMEM((3, xs, sub, depth), f32),
            field, field, block, field,
            pltpu.VMEM((2, 2, zts, rows, LANES), f32),
            pltpu.VMEM((3, 2, xs, zts, 3 * rhs, LANES), f32),
            pltpu.VMEM((2, 2, xs, zts, 3 * rhs, LANES), f32),
            pltpu.VMEM((2, xs // 2, zts, 3 * rhs, LANES), f32),
            pltpu.VMEM((2, sub, depth), jnp.int32),
            pltpu.VMEM((2, xs, depth), jnp.int32),
            pltpu.VMEM((2, xs, depth), jnp.int32),
            pltpu.VMEM((xs, sub, LANES), jnp.int32),
            pltpu.VMEM((n_row, 3 * rhs, LANES), f32),
            pltpu.VMEM((6, 3 * rhs, LANES), f32),
            dma((12,)),
            dma((xs,)),
            dma((20,)),
            dma((20,)),
            dma((2, 2, xs)),
            dma((2, 2, xs)),
            dma((2, xs // 2)),
            dma((2, xs // 2)),
            dma((n_row - 1,)),
            dma((n_row - 1,)),
        ],
        compiler_params=pltpu.CompilerParams(
            collective_id=0, has_side_effects=True, vmem_limit_bytes=52 * 2**20
        ),
    )(load, diagonal_block, coupling, aggregates, coarse_inverse)
    return pl.pallas_call(
        deliver,
        out_shape=jax.ShapeDtypeStruct(load.shape, f32),
        in_specs=[pl.BlockSpec(memory_space=pl.ANY)],
        out_specs=pl.BlockSpec(memory_space=pl.ANY),
        scratch_shapes=[dma((xs * zts,))],
        compiler_params=pltpu.CompilerParams(vmem_limit_bytes=2**20),
    )(tiles)


def solution(mesh):
    in_specs = (
        P(None, None, "row", "col", "dep"),
        P(None, None, "row", "col", "dep"),
        P(None, None, None, "row", "col", "dep"),
        P("row", "col", "dep"),
        P("col", "dep", None, None),
    )
    out_specs = P(None, None, "row", "col", "dep")
    return jax.shard_map(
        functools.partial(on_device, mesh.shape["row"], mesh.shape["col"]),
        mesh=mesh, in_specs=in_specs, out_specs=out_specs, check_vma=False,
    )
```
